32 devices in a mesh: ctx: 4 (over y, x), tp: 8 (over z, core).
Axes of the slice: x: 2, y: 2, z: 4, core: 2. Of those that a mesh axis runs over, the one named last changes fastest.
Arguments:
- normed_rows: bfloat16 [3072, 4096], P(('ctx', 'tp')), may hold values from -6 to 6
- out_grad: bfloat16 [3072, 4096], P(('ctx', 'tp')), may hold values from -6 to 6
- inner_weight: bfloat16 [2, 4096, 2048], P(None, None, 'tp'), may hold values from -0.09375 to 0.09375
- state_weight: bfloat16 [4096, 256], replicated, may hold values from -0.09375 to 0.09375
- step_weight: bfloat16 [4096, 16], P(None, 'tp'), may hold values from -0.09375 to 0.09375
- conv_inner: float32 [4, 2048], P(None, 'tp'), may hold values from -3 to 3
- conv_state: float32 [4, 256], replicated, may hold values from -3 to 3
- step_bias: float32 [16], P('tp'), may hold values from -4 to -1
- decay_log: float32 [16], P('tp')
- norm_gain: float32 [2048], P('tp'), may hold values from 0.1 to 1.9
- out_weight: bfloat16 [2048, 4096], P('tp'), may hold values from -0.125 to 0.125
Outputs:
- input_grad: bfloat16 [3072, 4096], P(('ctx', 'tp'))
The draws below stay inside these ranges and needn't reach their ends.
All inputs are finite; a program needn't handle non-finite values.
Results may differ from the reference program's by a relative error of at most 0.0095.
Values may be sent and summed in bfloat16 or wider, within the bound.
No kernel may reach another device: no remote copies, remote signals or barrier semaphores. Data moves between devices by JAX's collectives and lax.ppermute only.
A program may use at most 128 MiB of HBM per device.

```python
import math
import jax
import jax.numpy as jnp
from jax import lax

D = 4096
HEAD_DIM = 128
STATE = 128
CONV = 4
HEADS = 16
CHANNELS = 2048
SEQ = 3072


def draw_decay_log(key, part):
    pick_key, slow_key, fast_key = jax.random.split(key, 3)
    share = 0.5
    slow = jax.random.uniform(pick_key, (HEADS,), jnp.float32) < share
    slow_rate = jnp.exp(jax.random.uniform(slow_key, (HEADS,), jnp.float32, jnp.log(0.2), jnp.log(2.0))) / SEQ
    fast_rate = jnp.exp(jax.random.uniform(fast_key, (HEADS,), jnp.float32, jnp.log(0.05), -0.5))
    return jnp.log(jnp.where(slow, slow_rate, fast_rate)).astype(jnp.float32)


def shard_levels(stream_key, dims, cuts, low, largest):
    gain = 1.0
    for axis_at, parts in cuts:
        steps = jax.random.uniform(jax.random.fold_in(jax.random.fold_in(stream_key, 6), axis_at), (parts,), jnp.float32, low / len(cuts), largest / len(cuts))
        gain = gain * jnp.repeat(jnp.exp(steps), dims[axis_at] // parts).reshape((-1,) + (1,) * (len(dims) - 1 - axis_at))
    return gain


def centred(key, dims, scale, reach, pieces=(), held_as=jnp.bfloat16):
    array = jax.random.normal(key, dims, jnp.float32) * scale
    if len(pieces) > 0:
        array = shard_levels(key, dims, pieces, -0.22, 0.18) * array
    return jnp.clip(array, min=-reach, max=reach).astype(held_as)


def setup_inputs(seed: int = 0) -> dict:
    key_of = jax.random.split(jax.random.key(seed), 12)
    normed_rows = centred(key_of[0], (SEQ, D), 1.0, 6.0, ((0, 32),))
    out_grad = centred(key_of[1], (SEQ, D), 1.0, 6.0, ((0, 32),))
    inner_weight = centred(key_of[2], (2, D, CHANNELS), D ** -0.5, 0.09375, ((2, 8),))
    state_weight = centred(key_of[3], (D, 2 * STATE), D ** -0.5, 0.09375)
    step_weight = centred(key_of[4], (D, HEADS), D ** -0.5, 0.09375, ((1, 8),))
    conv_inner = centred(key_of[5], (CONV, CHANNELS), CONV ** -0.5, 3.0, ((1, 8),), jnp.float32)
    conv_state = centred(key_of[6], (CONV, 2 * STATE), CONV ** -0.5, 3.0, (), jnp.float32)
    step_bias = jnp.clip(-4.0 + 3.0 * jax.random.uniform(key_of[7], (HEADS,), jnp.float32) ** shard_levels(key_of[7], (HEADS,), ((0, 8),), -0.2, 0.2), -4.0, -1.0)
    decay_log = draw_decay_log(jax.random.fold_in(key_of[11], 71), 0)
    norm_gain = jnp.clip(1.0 + 0.18 * jax.random.normal(key_of[9], (CHANNELS,), jnp.float32), 0.1, 1.9)
    out_weight = centred(key_of[10], (CHANNELS, D), CHANNELS ** -0.5, 0.125, ((0, 8),))
    return {"normed_rows": normed_rows, "out_grad": out_grad, "inner_weight": inner_weight, "state_weight": state_weight, "step_weight": step_weight, "conv_inner": conv_inner, "conv_state": conv_state, "step_bias": step_bias, "decay_log": decay_log, "norm_gain": norm_gain, "out_weight": out_weight}


EPSILON = 1e-05
EXACT = lax.Precision.HIGHEST

def decay_table(log_decay):
    running = jnp.cumsum(log_decay, axis=0)
    length = log_decay.shape[0]
    causal = (lax.broadcasted_iota(jnp.int32, (length, length), 0) >= lax.broadcasted_iota(jnp.int32, (length, length), 1)).astype(jnp.float32)
    spread_log = running.T[:, :, None] - running.T[:, None, :]
    return (running, jnp.exp(jnp.minimum(spread_log, 0.0)) * causal)

def within_shard(inner_act, step_size, log_decay, b_rows, c_rows, entering):
    running, decays = decay_table(log_decay)
    scores = jnp.dot(c_rows, b_rows.T, precision=EXACT)
    weights = decays * scores[None] * step_size.T[:, None, :]
    local_part = jnp.einsum('hts,shp->thp', weights, inner_act, precision=EXACT)
    carried = jnp.einsum('tn,hpn->thp', c_rows, entering, precision=EXACT) * jnp.exp(running)[:, :, None]
    return local_part + carried

def leaving_state(inner_act, step_size, log_decay, b_rows, entering):
    running = jnp.cumsum(log_decay, axis=0)
    weights = jnp.exp(running[-1][None, :] - running) * step_size
    own_state = jnp.einsum('th,thp,tn->hpn', weights, inner_act, b_rows, precision=EXACT)
    return jnp.exp(running[-1])[:, None, None] * entering + own_state

def scan_blocks(inner_act, step_size, log_decay, b_rows, c_rows):
    length = inner_act.shape[0]
    block_len = math.gcd(length, 128)
    block_count = length // block_len
    head_count = inner_act.shape[1]

    def advance(entering, blocks):
        act_part, size_part, decay_part, brow_part, crow_part = blocks
        output = within_shard(act_part, size_part, decay_part, brow_part, crow_part, entering)
        return (leaving_state(act_part, size_part, decay_part, brow_part, entering), output)
    initial = jnp.zeros((head_count, inner_act.shape[2], b_rows.shape[1]), jnp.float32)
    blocks = (inner_act.reshape(block_count, block_len, head_count, -1), step_size.reshape(block_count, block_len, head_count), log_decay.reshape(block_count, block_len, head_count), b_rows.reshape(block_count, block_len, -1), c_rows.reshape(block_count, block_len, -1))
    _, outputs = lax.scan(advance, initial, blocks)
    return outputs.reshape(length, head_count, -1)

def mixer_core(gate_value, conv_in, step_raw, conv_inner, conv_state, step_bias, decay_log, norm_gain):
    length = conv_in.shape[0]
    kernel = jnp.concatenate([conv_inner, conv_state], axis=1)
    padded = jnp.concatenate([jnp.zeros((CONV - 1, conv_in.shape[1]), jnp.float32), conv_in], axis=0)
    blended = jnp.zeros_like(conv_in)
    for offset in range(CONV):
        blended = blended + kernel[offset] * padded[offset:offset + length]
    active = jax.nn.silu(blended)
    inner_act = active[:, :CHANNELS].reshape(length, HEADS, HEAD_DIM)
    b_rows = active[:, CHANNELS:CHANNELS + STATE]
    c_rows = active[:, CHANNELS + STATE:]
    step_size = jax.nn.softplus(step_raw + step_bias)
    log_decay = -step_size * jnp.exp(decay_log)
    scan_out = scan_blocks(inner_act, step_size, log_decay, b_rows, c_rows).reshape(length, CHANNELS)
    gated_out = scan_out * jax.nn.silu(gate_value)
    mean_square = lax.optimization_barrier(jnp.mean(gated_out * gated_out, axis=1, keepdims=True))
    return gated_out * lax.rsqrt(mean_square + EPSILON) * norm_gain

def reference(normed_rows, out_grad, inner_weight, state_weight, step_weight, conv_inner, conv_state, step_bias, decay_log, norm_gain, out_weight):
    gate_raw = jnp.dot(normed_rows, inner_weight[0], preferred_element_type=jnp.float32).astype(jnp.bfloat16)
    inner_raw = jnp.dot(normed_rows, inner_weight[1], preferred_element_type=jnp.float32).astype(jnp.bfloat16)
    state_raw = jnp.dot(normed_rows, state_weight, preferred_element_type=jnp.float32).astype(jnp.bfloat16)
    step_raw = jnp.dot(normed_rows, step_weight, preferred_element_type=jnp.float32).astype(jnp.bfloat16)
    conv_in = jnp.concatenate([inner_raw, state_raw], axis=1).astype(jnp.float32)
    out_local = jnp.dot(out_grad, out_weight.T, preferred_element_type=jnp.float32)

    def forward(gate_value, conv_value, step_value):
        return mixer_core(gate_value, conv_value, step_value, conv_inner, conv_state, step_bias, decay_log, norm_gain)
    _, pull_back = jax.vjp(forward, gate_raw.astype(jnp.float32), conv_in, step_raw.astype(jnp.float32))
    d_gate, d_conv, d_step = pull_back(out_local)
    input_term = jnp.dot(d_gate.astype(jnp.bfloat16), inner_weight[0].T, preferred_element_type=jnp.float32)
    input_term = input_term + jnp.dot(d_conv[:, :CHANNELS].astype(jnp.bfloat16), inner_weight[1].T, preferred_element_type=jnp.float32)
    input_term = input_term + jnp.dot(d_step.astype(jnp.bfloat16), step_weight.T, preferred_element_type=jnp.float32)
    input_term = input_term + jnp.dot(d_conv[:, CHANNELS:], state_weight.astype(jnp.float32).T, precision=EXACT, preferred_element_type=jnp.float32)
    return input_term.astype(jnp.bfloat16)
```

```python
import math
from functools import partial

import jax
import jax.numpy as jnp
from jax import lax
from jax.experimental import pallas as pl
from jax.experimental.pallas import tpu as pltpu
from jax.sharding import PartitionSpec as P

HEAD_DIM = 128
STATE = 128
CONV = 4
LANES = 128
PAD = 8
EPSILON = 1e-05
EXACT = lax.Precision.HIGHEST
F32 = jnp.float32
BF16 = jnp.bfloat16
PARAMS = dict(compiler_params=pltpu.CompilerParams(vmem_limit_bytes=16 * 1024 * 1024))


def dot(a, b, over=(1, 0), precision=None):
    return lax.dot_general(
        a, b, (((over[0],), (over[1],)), ((), ())), precision=precision, preferred_element_type=F32
    )


def triangle(size, keep):
    rows = lax.broadcasted_iota(jnp.int32, (size, size), 0)
    columns = lax.broadcasted_iota(jnp.int32, (size, size), 1)
    return keep(rows, columns)


def head(h):
    return slice(h * HEAD_DIM, (h + 1) * HEAD_DIM)


def forward_local(
    heads, block, proj, tail, kern, bias, rate,
    act_out, scaled_out, slope_out, step_out, run_out, sig_out, decay_out, table_out, diag_out, states_out,
    own_out, ext,
):
    length = proj.shape[0]
    width = heads * HEAD_DIM
    conv_width = width + 2 * STATE
    ext[0:PAD, :] = tail[...].astype(F32)
    ext[PAD:, :] = proj[:, width : width + conv_width].astype(F32)
    causal = triangle(block, lambda i, j: i >= j)
    lower = causal.astype(F32)
    state = [jnp.zeros((HEAD_DIM, STATE), F32) for _ in range(heads)]
    for k in range(length // block):
        rows = slice(k * block, (k + 1) * block)
        first = k * block + PAD - (CONV - 1)
        value = kern[0:1, :] * ext[first : first + block, :]
        for j in range(1, CONV):
            value = value + kern[j : j + 1, :] * ext[first + j : first + j + block, :]
        sigmoid = 1.0 / (1.0 + jnp.exp(-value))
        act = value * sigmoid
        act_out[rows, :] = act.astype(BF16)
        slope_out[rows, :] = sigmoid * (1.0 + value * (1.0 - sigmoid))
        raw = proj[rows, width + conv_width :].astype(F32) + bias[...]
        grown = jnp.exp(-jnp.abs(raw))
        step = jnp.maximum(raw, 0.0) + jnp.log1p(grown)
        step_out[rows, :] = step
        sig_out[rows, :] = jnp.where(raw >= 0.0, 1.0, grown) / (1.0 + grown)
        run = dot(lower, -step * rate[...], precision=EXACT)
        run_out[rows, :] = run
        run_t = run.T
        b_rows = act[:, width : width + STATE]
        c_rows = act[:, width + STATE :]
        scores = dot(c_rows, b_rows, (1, 1), EXACT)
        for h in range(heads):
            at = k * heads + h
            col = run[:, h : h + 1]
            decay = jnp.where(causal, jnp.exp(jnp.minimum(col - run_t[h : h + 1, :], 0.0)), 0.0)
            table = decay * scores
            scaled = act[:, head(h)] * step[:, h : h + 1]
            scaled_out[rows, head(h)] = scaled.astype(BF16)
            decay_out[rows, head(h)] = decay.astype(BF16)
            table_out[rows, head(h)] = table.astype(BF16)
            diag_out[rows, head(h)] = dot(table, scaled, precision=EXACT)
            states_out[at * HEAD_DIM : (at + 1) * HEAD_DIM, :] = state[h]
            last = run[block - 1 : block, h : h + 1]
            state[h] = jnp.exp(last) * state[h] + dot(
                jnp.exp(last - col) * scaled, b_rows, (0, 0), EXACT
            )
    for h in range(heads):
        own_out[head(h), :] = state[h]


def forward_carried(
    heads, block, proj, act, run, diag, states, weights, *refs,
):
    received = refs[:-6]
    gated_out, silu_out, slope_out, carried_out, states_out, sums_out = refs[-6:]
    length = proj.shape[0]
    width = heads * HEAD_DIM
    entering = []
    for h in range(heads):
        total = jnp.zeros((HEAD_DIM, STATE), F32)
        for i, part in enumerate(received):
            total = total + weights[i * heads + h : i * heads + h + 1, :] * part[head(h), :]
        entering.append(total)
    base = jnp.zeros((1, LANES), F32)
    ones = jnp.ones((8, width), F32)
    for k in range(length // block):
        rows = slice(k * block, (k + 1) * block)
        r = run[rows, :]
        grow = jnp.exp(r)
        reach = jnp.exp(base)
        c_rows = act[rows, width + STATE :].astype(F32)
        for h in range(heads):
            at = k * heads + h
            here = slice(at * HEAD_DIM, (at + 1) * HEAD_DIM)
            state = states[here, :] + reach[:, h : h + 1] * entering[h]
            states_out[here, :] = state.astype(BF16)
            carried = grow[:, h : h + 1] * dot(c_rows, state, (1, 1), EXACT)
            carried_out[rows, head(h)] = carried.astype(BF16)
            out = diag[rows, head(h)] + carried
            gate = proj[rows, head(h)].astype(F32)
            sigmoid = 1.0 / (1.0 + jnp.exp(-gate))
            silu = gate * sigmoid
            silu_out[rows, head(h)] = silu
            gated_out[rows, head(h)] = out * silu
            slope_out[rows, head(h)] = out * sigmoid * (1.0 + gate * (1.0 - sigmoid))
        base = base + r[block - 1 : block, :]
        gated = gated_out[rows, :]
        sums_out[:, rows] = dot(ones, gated * gated, (1, 1), EXACT)


def project_back(grads, weight, gain, gated, sums, local_out, sums_out):
    local = dot(grads[...], weight[...], (1, 1))
    local_out[...] = local
    ones = jnp.ones((8, local.shape[1]), F32)
    cross = dot(ones, gain[...] * local * gated[...], (1, 1), EXACT)
    upper = lax.broadcasted_iota(jnp.int32, cross.shape, 0) < 4
    sums_out[...] = jnp.where(upper, sums[...], cross)


def backward_gate(heads, block, total_width, local, gain, gated, silu, slope, act, run, *refs):
    parts = refs[:-5]
    dgate_out, cot_out, grown_out, blocks_out, own_out = refs[-5:]
    length = local.shape[0]
    width = heads * HEAD_DIM
    pick = lax.broadcasted_iota(jnp.int32, (8, LANES), 0)
    own = [jnp.zeros((HEAD_DIM, STATE), F32) for _ in range(heads)]
    base = jnp.zeros((1, LANES), F32)
    for k in range(length // block):
        rows = slice(k * block, (k + 1) * block)
        sums = parts[0][:, rows]
        for part in parts[1:]:
            sums = sums + part[:, rows]
        square = dot(sums, (pick == 0).astype(F32), (0, 0), EXACT) / total_width
        cross = dot(sums, (pick == 4).astype(F32), (0, 0), EXACT) / total_width
        inverse = lax.rsqrt(square + EPSILON)
        cross = cross * (inverse * inverse * inverse)
        r = run[rows, :]
        grow = jnp.exp(r)
        reach = jnp.exp(base)
        c_rows = act[rows, width + STATE :]
        for h in range(heads):
            at = k * heads + h
            d_gated = inverse * (gain[:, head(h)] * local[rows, head(h)]) - gated[rows, head(h)] * cross
            dgate_out[rows, head(h)] = (d_gated * slope[rows, head(h)]).astype(BF16)
            cot = d_gated * silu[rows, head(h)]
            cot_out[rows, head(h)] = cot.astype(BF16)
            grown = (grow[:, h : h + 1] * cot).astype(BF16)
            grown_out[rows, head(h)] = grown
            entering = dot(grown, c_rows, (0, 0))
            blocks_out[at * HEAD_DIM : (at + 1) * HEAD_DIM, :] = entering
            own[h] = own[h] + reach[:, h : h + 1] * entering
        base = base + r[block - 1 : block, :]
    for h in range(heads):
        own_out[head(h), :] = own[h]


def backward_local(
    heads, block, cot, grown, act, scaled, decays, table, states, carried, u_out, dbc_out, decay_out
):
    length = cot.shape[0]
    width = heads * HEAD_DIM
    before = triangle(block, lambda i, j: i > j)
    upper = triangle(block, lambda i, j: i <= j).astype(BF16)
    lane = lax.broadcasted_iota(jnp.int32, (block, LANES), 1)
    for k in range(length // block):
        rows = slice(k * block, (k + 1) * block)
        b_rows = act[rows, width : width + STATE]
        c_rows = act[rows, width + STATE :]
        d_brows = jnp.zeros((block, STATE), F32)
        d_crows = jnp.zeros((block, STATE), F32)
        decay = jnp.zeros((block, LANES), F32)
        for h in range(heads):
            at = k * heads + h
            g = cot[rows, head(h)]
            weights = table[rows, head(h)]
            inner = dot(g, scaled[rows, head(h)], (1, 1))
            pairs = (decays[rows, head(h)].astype(F32) * inner).astype(BF16)
            mixed = (weights.astype(F32) * inner).astype(BF16)
            d_crows = d_crows + dot(pairs, b_rows)
            d_crows = d_crows + dot(grown[rows, head(h)], states[at * HEAD_DIM : (at + 1) * HEAD_DIM, :])
            d_brows = d_brows + dot(pairs, c_rows, (0, 0))
            u_out[rows, head(h)] = dot(weights, g, (0, 0))
            through = (g.astype(F32) * carried[rows, head(h)].astype(F32)).astype(BF16)
            spread = jnp.where(before, dot(upper, mixed), 0.0) + dot(upper, through)
            decay = jnp.where(lane == h, jnp.sum(spread, axis=1, keepdims=True), decay)
        dbc_out[rows, :STATE] = d_brows
        dbc_out[rows, STATE:] = d_crows
        decay_out[rows, :] = decay


def backward_carried(
    heads, block, dgate, act, scaled, slope, step, run, sig, rate, kern, states, blocks, u, dbc, decay, weights,
    *refs,
):
    received = refs[:-4]
    cat_out, end_out, tail_out, scr = refs[-4:]
    length = dgate.shape[0]
    width = heads * HEAD_DIM
    conv_width = width + 2 * STATE
    strict = triangle(block, lambda i, j: i > j).astype(BF16)
    lane = lax.broadcasted_iota(jnp.int32, (block, LANES), 1)
    scr[0:PAD, :] = jnp.zeros((PAD, conv_width), F32)
    scr[PAD + length :, :] = jnp.zeros((PAD, conv_width), F32)
    cat_out[:, :width] = dgate[...]
    leaving = []
    for h in range(heads):
        total = jnp.zeros((HEAD_DIM, STATE), F32)
        for i, part in enumerate(received):
            total = total + weights[i * heads + h : i * heads + h + 1, :] * part[head(h), :]
        leaving.append(total)
    for k in reversed(range(length // block)):
        rows = slice(k * block, (k + 1) * block)
        into = slice(PAD + k * block, PAD + (k + 1) * block)
        r = run[rows, :]
        last = r[block - 1 : block, :]
        shrink = jnp.exp(last - r)
        whole = jnp.exp(last)
        b_rows = act[rows, width : width + STATE]
        d_brows = dbc[rows, :STATE]
        d_step = jnp.zeros((block, LANES), F32)
        for h in range(heads):
            at = k * heads + h
            here = slice(at * HEAD_DIM, (at + 1) * HEAD_DIM)
            cot_state = leaving[h].astype(BF16)
            past = shrink[:, h : h + 1] * dot(b_rows, cot_state, (1, 1))
            total = u[rows, head(h)] + past
            moved = scaled[rows, head(h)].astype(F32)
            d_brows = d_brows + dot((shrink[:, h : h + 1] * moved).astype(BF16), cot_state)
            kept = whole[:, h : h + 1] * leaving[h]
            constant = jnp.sum(
                jnp.sum(kept * states[here, :].astype(F32), axis=1, keepdims=True), axis=0, keepdims=True
            )
            spread = dot(strict, (moved * past).astype(BF16))
            d_decay = jnp.sum(spread, axis=1, keepdims=True) + constant + decay[rows, h : h + 1]
            direct = jnp.sum(act[rows, head(h)].astype(F32) * total, axis=1, keepdims=True)
            d_step = jnp.where(lane == h, direct - rate[:, h : h + 1] * d_decay, d_step)
            scr[into, head(h)] = step[rows, h : h + 1] * total * slope[rows, head(h)]
            leaving[h] = kept + blocks[here, :]
        scr[into, width : width + STATE] = d_brows * slope[rows, width : width + STATE]
        scr[into, width + STATE :] = dbc[rows, STATE:] * slope[rows, width + STATE :]
        cat_out[rows, width + conv_width :] = (d_step * sig[rows, :]).astype(BF16)
        value = kern[CONV - 1 : CONV, :] * scr[into, :]
        for j in range(1, CONV):
            value = value + kern[CONV - 1 - j : CONV - j, :] * scr[into.start + j : into.stop + j, :]
        cat_out[rows, width : width + conv_width] = value.astype(BF16)
        if k == length // block - 1:
            end_out[...] = value[block - PAD :, :]
    value = kern[CONV - 1 : CONV, :] * scr[0:PAD, :]
    for j in range(1, CONV):
        value = value + kern[CONV - 1 - j : CONV - j, :] * scr[j : PAD + j, :]
    tail_out[...] = value


def turned(value, axis, by):
    length = lax.axis_size(axis)
    return lax.ppermute(value, axis, [(i, (i + by) % length) for i in range(length)])


def paired(value, by):
    length = lax.axis_size("tp")
    return lax.ppermute(value, "tp", [(i, i ^ by) for i in range(length)])


def shifted(value, axis, by):
    length = lax.axis_size(axis)
    pairs = [(i, i + by) for i in range(length) if 0 <= i + by < length]
    return lax.ppermute(value, axis, pairs)


def shape(*dims, dtype=F32):
    return jax.ShapeDtypeStruct(dims, dtype)


def body(
    normed_rows, out_grad, inner_weight, state_weight, step_weight, conv_inner, conv_state,
    step_bias, decay_log, norm_gain, out_weight,
):
    width = inner_weight.shape[2]
    heads = step_bias.shape[0]
    members = lax.axis_size("tp")
    shards = lax.axis_size("ctx")
    mine = lax.axis_index("ctx")
    length = normed_rows.shape[0] * members
    block = math.gcd(length, 128)
    count = length // block
    conv_width = width + 2 * STATE

    weight_cat = jnp.concatenate(
        [inner_weight[0], inner_weight[1], state_weight, jnp.pad(step_weight, ((0, 0), (0, LANES - heads)))],
        axis=1,
    )
    kern = jnp.concatenate([conv_inner, conv_state], axis=1)
    bias = jnp.pad(step_bias, (0, LANES - heads))[None]
    rate = jnp.pad(jnp.exp(decay_log), (0, LANES - heads))[None]
    gain = norm_gain[None]

    rows_all = lax.all_gather(normed_rows, "tp", axis=0, tiled=True)
    proj = jnp.dot(rows_all, weight_cat, preferred_element_type=F32).astype(BF16)
    grads_all = lax.all_gather(out_grad, "tp", axis=0, tiled=True)

    tail = shifted(proj[length - PAD :, width : width + conv_width], "ctx", 1)
    act, scaled, slope, step, run, sig, decays, table, diag, states, own = pl.pallas_call(
        partial(forward_local, heads, block),
        out_shape=[
            shape(length, conv_width, dtype=BF16),
            shape(length, width, dtype=BF16),
            shape(length, conv_width),
            shape(length, LANES),
            shape(length, LANES),
            shape(length, LANES),
            shape(length, heads * block, dtype=BF16),
            shape(length, heads * block, dtype=BF16),
            shape(length, width),
            shape(count * heads * HEAD_DIM, STATE),
            shape(heads * HEAD_DIM, STATE),
        ],
        scratch_shapes=[pltpu.VMEM((PAD + length, conv_width), F32)],
        name="forward_local",
        **PARAMS,
    )(proj, tail, kern, bias, rate)

    ends = run.reshape(count, block, LANES)[:, block - 1, :heads]
    total_log = jnp.sum(ends, axis=0)
    message = jnp.concatenate([own, jnp.broadcast_to(jnp.pad(total_log, (0, LANES - heads)), (8, LANES))], axis=0)
    received = [turned(message, "ctx", by) for by in range(1, shards)]
    logs = [part[heads * HEAD_DIM, :heads] for part in received]
    entering_weights = []
    between = jnp.zeros((heads,), F32)
    for by in range(1, shards):
        entering_weights.append(jnp.where(mine >= by, jnp.exp(between), 0.0))
        between = between + jnp.where(mine >= by, logs[by - 1], 0.0)
    leaving_weights = []
    between = jnp.zeros((heads,), F32)
    for by in range(1, shards):
        leaving_weights.append(jnp.where(mine + by < shards, jnp.exp(between), 0.0))
        between = between + jnp.where(mine + by < shards, logs[shards - by - 1], 0.0)

    def spread(parts):
        flat = jnp.concatenate(parts)
        return jnp.broadcast_to(flat[:, None], (flat.shape[0], LANES))

    gated, silu, gate_slope, carried, full_states, squares = pl.pallas_call(
        partial(forward_carried, heads, block),
        out_shape=[
            shape(length, width),
            shape(length, width),
            shape(length, width),
            shape(length, width, dtype=BF16),
            shape(count * heads * HEAD_DIM, STATE, dtype=BF16),
            shape(8, length),
        ],
        name="forward_carried",
        **PARAMS,
    )(proj, act, run, diag, states, spread(entering_weights), *received)

    depth = out_grad.shape[1]
    local, sums = pl.pallas_call(
        project_back,
        grid=(count,),
        in_specs=[
            pl.BlockSpec((block, depth), lambda i: (i, 0)),
            pl.BlockSpec((width, depth), lambda i: (0, 0)),
            pl.BlockSpec((1, width), lambda i: (0, 0)),
            pl.BlockSpec((block, width), lambda i: (i, 0)),
            pl.BlockSpec((8, block), lambda i: (0, i)),
        ],
        out_specs=[
            pl.BlockSpec((block, width), lambda i: (i, 0)),
            pl.BlockSpec((8, block), lambda i: (0, i)),
        ],
        out_shape=[shape(length, width), shape(8, length)],
        name="project_back",
        **PARAMS,
    )(grads_all, out_weight, gain, gated, squares)

    sums = sums + paired(sums, 1)
    parts = [sums] + [turned(sums, "tp", by) for by in range(2, members, 2)]

    dgate, cot, grown, blocks, own_cot = pl.pallas_call(
        partial(backward_gate, heads, block, width * members),
        out_shape=[
            shape(length, width, dtype=BF16),
            shape(length, width, dtype=BF16),
            shape(length, width, dtype=BF16),
            shape(count * heads * HEAD_DIM, STATE),
            shape(heads * HEAD_DIM, STATE),
        ],
        name="backward_gate",
        **PARAMS,
    )(local, gain, gated, silu, gate_slope, act, run, *parts)

    returned = [turned(own_cot, "ctx", -by) for by in range(1, shards)]

    u, dbc, decay = pl.pallas_call(
        partial(backward_local, heads, block),
        out_shape=[shape(length, width), shape(length, 2 * STATE), shape(length, LANES)],
        name="backward_local",
        **PARAMS,
    )(cot, grown, act, scaled, decays, table, full_states, carried)

    cat, end, tail_cot = pl.pallas_call(
        partial(backward_carried, heads, block),
        out_shape=[
            shape(length, width + conv_width + LANES, dtype=BF16),
            shape(PAD, conv_width),
            shape(PAD, conv_width),
        ],
        scratch_shapes=[pltpu.VMEM((length + 2 * PAD, conv_width), F32)],
        name="backward_carried",
        **PARAMS,
    )(
        dgate, act, scaled, slope, step, run, sig, rate, kern, full_states, blocks, u, dbc, decay,
        spread(leaving_weights), *returned,
    )

    incoming = shifted(tail_cot, "ctx", -1)
    cat = lax.dynamic_update_slice(cat, (end + incoming).astype(BF16), (length - PAD, width))
    summed = dot(cat, weight_cat, (1, 1)).astype(BF16)
    return lax.psum_scatter(summed, "tp", scatter_dimension=0, tiled=True)


def solution(mesh):
    placed = (
        P(("ctx", "tp"), None),
        P(("ctx", "tp"), None),
        P(None, None, "tp"),
        P(),
        P(None, "tp"),
        P(None, "tp"),
        P(),
        P("tp"),
        P("tp"),
        P("tp"),
        P("tp", None),
    )
    return jax.shard_map(
        body, mesh=mesh, in_specs=placed, out_specs=P(("ctx", "tp"), None), check_vma=False
    )
```

```python
import math
from functools import partial

import jax
import jax.numpy as jnp
from jax import lax
from jax.experimental import pallas as pl
from jax.experimental.pallas import tpu as pltpu
from jax.sharding import PartitionSpec as P

HEAD_DIM = 128
STATE = 128
CONV = 4
LANES = 128
PAD = 8
EPSILON = 1e-05
EXACT = lax.Precision.HIGHEST
F32 = jnp.float32
BF16 = jnp.bfloat16
PARAMS = dict(
    compiler_params=pltpu.CompilerParams(vmem_limit_bytes=16 * 1024 * 1024),
    cost_estimate=pl.CostEstimate(flops=1000, bytes_accessed=1000, transcendentals=0),
)


def dot(a, b, over=(1, 0), precision=None):
    return lax.dot_general(
        a, b, (((over[0],), (over[1],)), ((), ())), precision=precision, preferred_element_type=F32
    )


def triangle(size, keep):
    rows = lax.broadcasted_iota(jnp.int32, (size, size), 0)
    columns = lax.broadcasted_iota(jnp.int32, (size, size), 1)
    return keep(rows, columns)


def head(h):
    return slice(h * HEAD_DIM, (h + 1) * HEAD_DIM)


def forward_local(
    heads, block, proj, tail, kern, bias, rate,
    act_out, scaled_out, slope_out, step_out, run_out, sig_out, decay_out, table_out, diag_out, states_out,
    own_out, ext,
):
    length = proj.shape[0]
    width = heads * HEAD_DIM
    conv_width = width + 2 * STATE
    ext[0:PAD, :] = tail[...].astype(F32)
    ext[PAD:, :] = proj[:, width : width + conv_width].astype(F32)
    causal = triangle(block, lambda i, j: i >= j)
    lower = causal.astype(F32)
    state = [jnp.zeros((HEAD_DIM, STATE), F32) for _ in range(heads)]
    for k in range(length // block):
        rows = slice(k * block, (k + 1) * block)
        first = k * block + PAD - (CONV - 1)
        value = kern[0:1, :] * ext[first : first + block, :]
        for j in range(1, CONV):
            value = value + kern[j : j + 1, :] * ext[first + j : first + j + block, :]
        sigmoid = 1.0 / (1.0 + jnp.exp(-value))
        act = value * sigmoid
        act_out[rows, :] = act.astype(BF16)
        slope_out[rows, :] = sigmoid * (1.0 + value * (1.0 - sigmoid))
        raw = proj[rows, width + conv_width :].astype(F32) + bias[...]
        grown = jnp.exp(-jnp.abs(raw))
        step = jnp.maximum(raw, 0.0) + jnp.log1p(grown)
        step_out[rows, :] = step
        sig_out[rows, :] = jnp.where(raw >= 0.0, 1.0, grown) / (1.0 + grown)
        run = dot(lower, -step * rate[...], precision=EXACT)
        run_out[rows, :] = run
        run_t = run.T
        b_rows = act[:, width : width + STATE]
        c_rows = act[:, width + STATE :]
        scores = dot(c_rows, b_rows, (1, 1), EXACT)
        for h in range(heads):
            at = k * heads + h
            col = run[:, h : h + 1]
            decay = jnp.where(causal, jnp.exp(jnp.minimum(col - run_t[h : h + 1, :], 0.0)), 0.0)
            table = decay * scores
            scaled = act[:, head(h)] * step[:, h : h + 1]
            scaled_out[rows, head(h)] = scaled.astype(BF16)
            decay_out[rows, head(h)] = decay.astype(BF16)
            table_out[rows, head(h)] = table.astype(BF16)
            diag_out[rows, head(h)] = dot(table, scaled, precision=EXACT)
            states_out[at * HEAD_DIM : (at + 1) * HEAD_DIM, :] = state[h]
            last = run[block - 1 : block, h : h + 1]
            state[h] = jnp.exp(last) * state[h] + dot(
                jnp.exp(last - col) * scaled, b_rows, (0, 0), EXACT
            )
    for h in range(heads):
        own_out[head(h), :] = state[h]


def forward_carried(
    heads, block, proj, act, run, diag, states, weights, *refs,
):
    received = refs[:-6]
    gated_out, silu_out, slope_out, carried_out, states_out, sums_out = refs[-6:]
    length = proj.shape[0]
    width = heads * HEAD_DIM
    entering = []
    for h in range(heads):
        total = jnp.zeros((HEAD_DIM, STATE), F32)
        for i, part in enumerate(received):
            total = total + weights[i * heads + h : i * heads + h + 1, :] * part[head(h), :]
        entering.append(total)
    base = jnp.zeros((1, LANES), F32)
    ones = jnp.ones((8, width), F32)
    for k in range(length // block):
        rows = slice(k * block, (k + 1) * block)
        r = run[rows, :]
        grow = jnp.exp(r)
        reach = jnp.exp(base)
        c_rows = act[rows, width + STATE :].astype(F32)
        for h in range(heads):
            at = k * heads + h
            here = slice(at * HEAD_DIM, (at + 1) * HEAD_DIM)
            state = states[here, :] + reach[:, h : h + 1] * entering[h]
            states_out[here, :] = state.astype(BF16)
            carried = grow[:, h : h + 1] * dot(c_rows, state, (1, 1), EXACT)
            carried_out[rows, head(h)] = carried.astype(BF16)
            out = diag[rows, head(h)] + carried
            gate = proj[rows, head(h)].astype(F32)
            sigmoid = 1.0 / (1.0 + jnp.exp(-gate))
            silu = gate * sigmoid
            silu_out[rows, head(h)] = silu
            gated_out[rows, head(h)] = out * silu
            slope_out[rows, head(h)] = out * sigmoid * (1.0 + gate * (1.0 - sigmoid))
        base = base + r[block - 1 : block, :]
        gated = gated_out[rows, :]
        sums_out[:, rows] = dot(ones, gated * gated, (1, 1), EXACT)


def token_sums(local, gain, gated, squares, sums_out):
    ones = jnp.ones((8, local.shape[1]), F32)
    cross = dot(ones, gain[...] * local[...] * gated[...], (1, 1), EXACT)
    upper = lax.broadcasted_iota(jnp.int32, cross.shape, 0) < 4
    sums_out[...] = jnp.where(upper, squares[...], cross)


def backward_gate(heads, block, total_width, local, gain, gated, silu, slope, act, run, *refs):
    parts = refs[:-5]
    dgate_out, cot_out, grown_out, blocks_out, own_out = refs[-5:]
    length = local.shape[0]
    width = heads * HEAD_DIM
    pick = lax.broadcasted_iota(jnp.int32, (8, LANES), 0)
    own = [jnp.zeros((HEAD_DIM, STATE), F32) for _ in range(heads)]
    base = jnp.zeros((1, LANES), F32)
    for k in range(length // block):
        rows = slice(k * block, (k + 1) * block)
        sums = parts[0][:, rows]
        for part in parts[1:]:
            sums = sums + part[:, rows]
        square = dot(sums, (pick == 0).astype(F32), (0, 0), EXACT) / total_width
        cross = dot(sums, (pick == 4).astype(F32), (0, 0), EXACT) / total_width
        inverse = lax.rsqrt(square + EPSILON)
        cross = cross * (inverse * inverse * inverse)
        r = run[rows, :]
        grow = jnp.exp(r)
        reach = jnp.exp(base)
        c_rows = act[rows, width + STATE :]
        for h in range(heads):
            at = k * heads + h
            d_gated = inverse * (gain[:, head(h)] * local[rows, head(h)]) - gated[rows, head(h)] * cross
            dgate_out[rows, head(h)] = (d_gated * slope[rows, head(h)]).astype(BF16)
            cot = d_gated * silu[rows, head(h)]
            cot_out[rows, head(h)] = cot.astype(BF16)
            grown = (grow[:, h : h + 1] * cot).astype(BF16)
            grown_out[rows, head(h)] = grown
            entering = dot(grown, c_rows, (0, 0))
            blocks_out[at * HEAD_DIM : (at + 1) * HEAD_DIM, :] = entering
            own[h] = own[h] + reach[:, h : h + 1] * entering
        base = base + r[block - 1 : block, :]
    for h in range(heads):
        own_out[head(h), :] = own[h]


def backward_local(
    heads, block, cot, grown, act, scaled, decays, table, states, carried, u_out, dbc_out, decay_out
):
    length = cot.shape[0]
    width = heads * HEAD_DIM
    before = triangle(block, lambda i, j: i > j)
    upper = triangle(block, lambda i, j: i <= j).astype(BF16)
    lane = lax.broadcasted_iota(jnp.int32, (block, LANES), 1)
    for k in range(length // block):
        rows = slice(k * block, (k + 1) * block)
        b_rows = act[rows, width : width + STATE]
        c_rows = act[rows, width + STATE :]
        d_brows = jnp.zeros((block, STATE), F32)
        d_crows = jnp.zeros((block, STATE), F32)
        decay = jnp.zeros((block, LANES), F32)
        for h in range(heads):
            at = k * heads + h
            g = cot[rows, head(h)]
            weights = table[rows, head(h)]
            inner = dot(g, scaled[rows, head(h)], (1, 1))
            pairs = (decays[rows, head(h)].astype(F32) * inner).astype(BF16)
            mixed = (weights.astype(F32) * inner).astype(BF16)
            d_crows = d_crows + dot(pairs, b_rows)
            d_crows = d_crows + dot(grown[rows, head(h)], states[at * HEAD_DIM : (at + 1) * HEAD_DIM, :])
            d_brows = d_brows + dot(pairs, c_rows, (0, 0))
            u_out[rows, head(h)] = dot(weights, g, (0, 0))
            through = (g.astype(F32) * carried[rows, head(h)].astype(F32)).astype(BF16)
            spread = jnp.where(before, dot(upper, mixed), 0.0) + dot(upper, through)
            decay = jnp.where(lane == h, jnp.sum(spread, axis=1, keepdims=True), decay)
        dbc_out[rows, :STATE] = d_brows
        dbc_out[rows, STATE:] = d_crows
        decay_out[rows, :] = decay


def backward_carried(
    heads, block, dgate, act, scaled, slope, step, run, sig, rate, kern, states, blocks, u, dbc, decay, weights,
    *refs,
):
    received = refs[:-4]
    cat_out, end_out, tail_out, scr = refs[-4:]
    length = dgate.shape[0]
    width = heads * HEAD_DIM
    conv_width = width + 2 * STATE
    strict = triangle(block, lambda i, j: i > j).astype(BF16)
    lane = lax.broadcasted_iota(jnp.int32, (block, LANES), 1)
    scr[0:PAD, :] = jnp.zeros((PAD, conv_width), F32)
    scr[PAD + length :, :] = jnp.zeros((PAD, conv_width), F32)
    cat_out[:, :width] = dgate[...]
    leaving = []
    for h in range(heads):
        total = jnp.zeros((HEAD_DIM, STATE), F32)
        for i, part in enumerate(received):
            total = total + weights[i * heads + h : i * heads + h + 1, :] * part[head(h), :]
        leaving.append(total)
    for k in reversed(range(length // block)):
        rows = slice(k * block, (k + 1) * block)
        into = slice(PAD + k * block, PAD + (k + 1) * block)
        r = run[rows, :]
        last = r[block - 1 : block, :]
        shrink = jnp.exp(last - r)
        whole = jnp.exp(last)
        b_rows = act[rows, width : width + STATE]
        d_brows = dbc[rows, :STATE]
        d_step = jnp.zeros((block, LANES), F32)
        for h in range(heads):
            at = k * heads + h
            here = slice(at * HEAD_DIM, (at + 1) * HEAD_DIM)
            cot_state = leaving[h].astype(BF16)
            past = shrink[:, h : h + 1] * dot(b_rows, cot_state, (1, 1))
            total = u[rows, head(h)] + past
            moved = scaled[rows, head(h)].astype(F32)
            d_brows = d_brows + dot((shrink[:, h : h + 1] * moved).astype(BF16), cot_state)
            kept = whole[:, h : h + 1] * leaving[h]
            constant = jnp.sum(
                jnp.sum(kept * states[here, :].astype(F32), axis=1, keepdims=True), axis=0, keepdims=True
            )
            spread = dot(strict, (moved * past).astype(BF16))
            d_decay = jnp.sum(spread, axis=1, keepdims=True) + constant + decay[rows, h : h + 1]
            direct = jnp.sum(act[rows, head(h)].astype(F32) * total, axis=1, keepdims=True)
            d_step = jnp.where(lane == h, direct - rate[:, h : h + 1] * d_decay, d_step)
            scr[into, head(h)] = step[rows, h : h + 1] * total * slope[rows, head(h)]
            leaving[h] = kept + blocks[here, :]
        scr[into, width : width + STATE] = d_brows * slope[rows, width : width + STATE]
        scr[into, width + STATE :] = dbc[rows, STATE:] * slope[rows, width + STATE :]
        cat_out[rows, width + conv_width :] = (d_step * sig[rows, :]).astype(BF16)
        value = kern[CONV - 1 : CONV, :] * scr[into, :]
        for j in range(1, CONV):
            value = value + kern[CONV - 1 - j : CONV - j, :] * scr[into.start + j : into.stop + j, :]
        cat_out[rows, width : width + conv_width] = value.astype(BF16)
        if k == length // block - 1:
            end_out[...] = value[block - PAD :, :]
    value = kern[CONV - 1 : CONV, :] * scr[0:PAD, :]
    for j in range(1, CONV):
        value = value + kern[CONV - 1 - j : CONV - j, :] * scr[j : PAD + j, :]
    tail_out[...] = value


def turned(value, axis, by):
    length = lax.axis_size(axis)
    return lax.ppermute(value, axis, [(i, (i + by) % length) for i in range(length)])


def paired(value, by):
    length = lax.axis_size("tp")
    return lax.ppermute(value, "tp", [(i, i ^ by) for i in range(length)])


def shifted(value, axis, by):
    length = lax.axis_size(axis)
    pairs = [(i, i + by) for i in range(length) if 0 <= i + by < length]
    return lax.ppermute(value, axis, pairs)


def after(value, token):
    return value + (token[0, 0] * 0).astype(value.dtype)


def halves(held):
    return ((0, held // 2), (held // 2, held - held // 2))


def ring_gather(parts, consume, result):
    chips = lax.axis_size("tp") // 2
    index = lax.axis_index("tp")
    chip, core = index // 2, index % 2
    arrived = []
    for step in range(chips):
        beside = [paired(part, 1) for part in parts]
        source = (chip - step) % chips
        owners = (source * 2 + core, source * 2 + 1 - core)
        if step < chips - 1:
            following = [turned(part, "tp", 2) for part in parts]
            result = consume(result, parts + beside, owners, None)
            parts = following
            arrived.append(parts)
        else:
            for i in range(len(parts)):
                result = consume(result, [parts[i], beside[i]], owners, i)
    return result, arrived


def multiply_into(weight, over, held, dtype):
    cuts = halves(held)

    def consume(result, rows, owners, only):
        product = dot(jnp.concatenate(rows, axis=0), weight, over).astype(dtype)
        at, size = (0, held) if only is None else cuts[only]
        for i, owner in enumerate(owners):
            piece = product[i * size : (i + 1) * size]
            result = lax.dynamic_update_slice(result, piece, (owner * held + at, 0))
        return result

    return consume


def ring_scatter(cat_parts, weight, held):
    chips = lax.axis_size("tp") // 2
    index = lax.axis_index("tp")
    chip, core = index // 2, index % 2
    travelling = [None, None]
    events = []
    for step in range(chips):
        target = (chip - 1 - step) % chips
        for i, (at, size) in enumerate(halves(held)):
            rows = [
                lax.dynamic_slice(
                    cat_parts[i], ((target * 2 + side) * held + at, 0), (size, cat_parts[i].shape[1])
                )
                for side in (core, 1 - core)
            ]
            rows = jnp.concatenate(rows, axis=0)
            if step > 0:
                rows = after(rows, events[max(2 * step + i - 3, 0)])
            product = dot(rows, weight, (1, 1)).astype(BF16)
            total = product[:size].astype(F32) + paired(product[size:], 1).astype(F32)
            if travelling[i] is not None:
                total = total + travelling[i].astype(F32)
            total = total.astype(BF16)
            travelling[i] = turned(total, "tp", 2) if step < chips - 1 else total
            events.append(travelling[i])
    return jnp.concatenate(travelling, axis=0)


def shape(*dims, dtype=F32):
    return jax.ShapeDtypeStruct(dims, dtype)


def body(
    normed_rows, out_grad, inner_weight, state_weight, step_weight, conv_inner, conv_state,
    step_bias, decay_log, norm_gain, out_weight,
):
    width = inner_weight.shape[2]
    heads = step_bias.shape[0]
    members = lax.axis_size("tp")
    shards = lax.axis_size("ctx")
    mine = lax.axis_index("ctx")
    length = normed_rows.shape[0] * members
    block = math.gcd(length, 128)
    count = length // block
    conv_width = width + 2 * STATE

    weight_cat = jnp.concatenate(
        [inner_weight[0], inner_weight[1], state_weight, jnp.pad(step_weight, ((0, 0), (0, LANES - heads)))],
        axis=1,
    )
    kern = jnp.concatenate([conv_inner, conv_state], axis=1)
    bias = jnp.pad(step_bias, (0, LANES - heads))[None]
    rate = jnp.pad(jnp.exp(decay_log), (0, LANES - heads))[None]
    gain = norm_gain[None]

    held, depth = normed_rows.shape
    cuts = halves(held)
    proj, rows_in = ring_gather(
        [normed_rows[at : at + size] for at, size in cuts],
        multiply_into(weight_cat, (1, 0), held, BF16),
        jnp.zeros((length, weight_cat.shape[1]), BF16),
    )
    local, grads_in = ring_gather(
        [after(out_grad[at : at + size], rows_in[-1][i]) for i, (at, size) in enumerate(cuts)],
        multiply_into(out_weight, (1, 1), held, F32),
        jnp.zeros((length, width), F32),
    )

    tail = shifted(proj[length - PAD :, width : width + conv_width], "ctx", 1)
    act, scaled, slope, step, run, sig, decays, table, diag, states, own = pl.pallas_call(
        partial(forward_local, heads, block),
        out_shape=[
            shape(length, conv_width, dtype=BF16),
            shape(length, width, dtype=BF16),
            shape(length, conv_width),
            shape(length, LANES),
            shape(length, LANES),
            shape(length, LANES),
            shape(length, heads * block, dtype=BF16),
            shape(length, heads * block, dtype=BF16),
            shape(length, width),
            shape(count * heads * HEAD_DIM, STATE),
            shape(heads * HEAD_DIM, STATE),
        ],
        scratch_shapes=[pltpu.VMEM((PAD + length, conv_width), F32)],
        name="forward_local",
        **PARAMS,
    )(proj, tail, kern, bias, rate)

    ends = run.reshape(count, block, LANES)[:, block - 1, :heads]
    total_log = jnp.sum(ends, axis=0)
    message = jnp.concatenate([own, jnp.broadcast_to(jnp.pad(total_log, (0, LANES - heads)), (8, LANES))], axis=0)
    received = [turned(message, "ctx", by) for by in range(1, shards)]
    logs = [part[heads * HEAD_DIM, :heads] for part in received]
    entering_weights = []
    between = jnp.zeros((heads,), F32)
    for by in range(1, shards):
        entering_weights.append(jnp.where(mine >= by, jnp.exp(between), 0.0))
        between = between + jnp.where(mine >= by, logs[by - 1], 0.0)
    leaving_weights = []
    between = jnp.zeros((heads,), F32)
    for by in range(1, shards):
        leaving_weights.append(jnp.where(mine + by < shards, jnp.exp(between), 0.0))
        between = between + jnp.where(mine + by < shards, logs[shards - by - 1], 0.0)

    def spread(parts):
        flat = jnp.concatenate(parts)
        return jnp.broadcast_to(flat[:, None], (flat.shape[0], LANES))

    gated, silu, gate_slope, carried, full_states, squares = pl.pallas_call(
        partial(forward_carried, heads, block),
        out_shape=[
            shape(length, width),
            shape(length, width),
            shape(length, width),
            shape(length, width, dtype=BF16),
            shape(count * heads * HEAD_DIM, STATE, dtype=BF16),
            shape(8, length),
        ],
        name="forward_carried",
        **PARAMS,
    )(proj, act, run, diag, states, spread(entering_weights), *received)

    sums = pl.pallas_call(token_sums, out_shape=shape(8, length), name="token_sums", **PARAMS)(
        local, gain, gated, squares
    )

    sums = sums + paired(sums, 1)
    parts = [sums] + [turned(sums, "tp", by) for by in range(2, members, 2)]

    dgate, cot, grown, blocks, own_cot = pl.pallas_call(
        partial(backward_gate, heads, block, width * members),
        out_shape=[
            shape(length, width, dtype=BF16),
            shape(length, width, dtype=BF16),
            shape(length, width, dtype=BF16),
            shape(count * heads * HEAD_DIM, STATE),
            shape(heads * HEAD_DIM, STATE),
        ],
        name="backward_gate",
        **PARAMS,
    )(local, gain, gated, silu, gate_slope, act, run, *parts)

    returned = [turned(own_cot, "ctx", -by) for by in range(1, shards)]

    u, dbc, decay = pl.pallas_call(
        partial(backward_local, heads, block),
        out_shape=[shape(length, width), shape(length, 2 * STATE), shape(length, LANES)],
        name="backward_local",
        **PARAMS,
    )(cot, grown, act, scaled, decays, table, full_states, carried)

    cat, end, tail_cot = pl.pallas_call(
        partial(backward_carried, heads, block),
        out_shape=[
            shape(length, width + conv_width + LANES, dtype=BF16),
            shape(PAD, conv_width),
            shape(PAD, conv_width),
        ],
        scratch_shapes=[pltpu.VMEM((length + 2 * PAD, conv_width), F32)],
        name="backward_carried",
        **PARAMS,
    )(
        dgate, act, scaled, slope, step, run, sig, rate, kern, full_states, blocks, u, dbc, decay,
        spread(leaving_weights), *returned,
    )

    incoming = shifted(tail_cot, "ctx", -1)
    whole = lax.dynamic_update_slice(cat, (end + incoming).astype(BF16), (length - PAD, width))
    return ring_scatter((cat, whole), weight_cat, held)


def solution(mesh):
    placed = (
        P(("ctx", "tp"), None),
        P(("ctx", "tp"), None),
        P(None, None, "tp"),
        P(),
        P(None, "tp"),
        P(None, "tp"),
        P(),
        P("tp"),
        P("tp"),
        P("tp"),
        P("tp", None),
    )
    return jax.shard_map(
        body, mesh=mesh, in_specs=placed, out_specs=P(("ctx", "tp"), None), check_vma=False
    )
```

```python
import math
from functools import partial

import jax
import jax.numpy as jnp
from jax import lax
from jax.experimental import pallas as pl
from jax.experimental.pallas import tpu as pltpu
from jax.sharding import PartitionSpec as P

HEAD_DIM = 128
STATE = 128
CONV = 4
LANES = 128
PAD = 8
EPSILON = 1e-05
EXACT = lax.Precision.HIGHEST
F32 = jnp.float32
BF16 = jnp.bfloat16
COST = pl.CostEstimate(flops=1000, bytes_accessed=1000, transcendentals=0)
VMEM_LIMIT = 16 * 1024 * 1024
PARAMS = dict(
    compiler_params=pltpu.CompilerParams(vmem_limit_bytes=16 * 1024 * 1024), cost_estimate=COST
)


def dot(a, b, over=(1, 0), precision=None):
    return lax.dot_general(
        a, b, (((over[0],), (over[1],)), ((), ())), precision=precision, preferred_element_type=F32
    )


def triangle(size, keep):
    rows = lax.broadcasted_iota(jnp.int32, (size, size), 0)
    columns = lax.broadcasted_iota(jnp.int32, (size, size), 1)
    return keep(rows, columns)


def head(h):
    return slice(h * HEAD_DIM, (h + 1) * HEAD_DIM)


def forward_local(
    heads, block, proj, tail, kern, bias, rate,
    act_out, scaled_out, slope_out, step_out, run_out, sig_out, decay_out, table_out, diag_out, states_out,
    own_out, ext,
):
    length = proj.shape[0]
    width = heads * HEAD_DIM
    conv_width = width + 2 * STATE
    ext[0:PAD, :] = tail[...].astype(F32)
    ext[PAD:, :] = proj[:, width : width + conv_width].astype(F32)
    causal = triangle(block, lambda i, j: i >= j)
    lower = causal.astype(F32)
    state = [jnp.zeros((HEAD_DIM, STATE), F32) for _ in range(heads)]
    for k in range(length // block):
        rows = slice(k * block, (k + 1) * block)
        first = k * block + PAD - (CONV - 1)
        value = kern[0:1, :] * ext[first : first + block, :]
        for j in range(1, CONV):
            value = value + kern[j : j + 1, :] * ext[first + j : first + j + block, :]
        sigmoid = 1.0 / (1.0 + jnp.exp(-value))
        act = value * sigmoid
        act_out[rows, :] = act.astype(BF16)
        slope_out[rows, :] = sigmoid * (1.0 + value * (1.0 - sigmoid))
        raw = proj[rows, width + conv_width :].astype(F32) + bias[...]
        grown = jnp.exp(-jnp.abs(raw))
        step = jnp.maximum(raw, 0.0) + jnp.log1p(grown)
        step_out[rows, :] = step
        sig_out[rows, :] = jnp.where(raw >= 0.0, 1.0, grown) / (1.0 + grown)
        run = dot(lower, -step * rate[...], precision=EXACT)
        run_out[rows, :] = run
        run_t = run.T
        b_rows = act[:, width : width + STATE]
        c_rows = act[:, width + STATE :]
        scores = dot(c_rows, b_rows, (1, 1), EXACT)
        for h in range(heads):
            at = k * heads + h
            col = run[:, h : h + 1]
            decay = jnp.where(causal, jnp.exp(jnp.minimum(col - run_t[h : h + 1, :], 0.0)), 0.0)
            table = decay * scores
            scaled = act[:, head(h)] * step[:, h : h + 1]
            scaled_out[rows, head(h)] = scaled.astype(BF16)
            decay_out[rows, head(h)] = decay.astype(BF16)
            table_out[rows, head(h)] = table.astype(BF16)
            diag_out[rows, head(h)] = dot(table, scaled, precision=EXACT)
            states_out[at * HEAD_DIM : (at + 1) * HEAD_DIM, :] = state[h]
            last = run[block - 1 : block, h : h + 1]
            state[h] = jnp.exp(last) * state[h] + dot(
                jnp.exp(last - col) * scaled, b_rows, (0, 0), EXACT
            )
    for h in range(heads):
        own_out[head(h), :] = state[h]


def forward_carried(
    heads, block, proj, act, run, diag, states, weights, *refs,
):
    received = refs[:-6]
    gated_out, silu_out, slope_out, carried_out, states_out, sums_out = refs[-6:]
    length = proj.shape[0]
    width = heads * HEAD_DIM
    entering = []
    for h in range(heads):
        total = jnp.zeros((HEAD_DIM, STATE), F32)
        for i, part in enumerate(received):
            total = total + weights[i * heads + h : i * heads + h + 1, :] * part[head(h), :]
        entering.append(total)
    base = jnp.zeros((1, LANES), F32)
    ones = jnp.ones((8, width), F32)
    for k in range(length // block):
        rows = slice(k * block, (k + 1) * block)
        r = run[rows, :]
        grow = jnp.exp(r)
        reach = jnp.exp(base)
        c_rows = act[rows, width + STATE :].astype(F32)
        for h in range(heads):
            at = k * heads + h
            here = slice(at * HEAD_DIM, (at + 1) * HEAD_DIM)
            state = states[here, :] + reach[:, h : h + 1] * entering[h]
            states_out[here, :] = state.astype(BF16)
            carried = grow[:, h : h + 1] * dot(c_rows, state, (1, 1), EXACT)
            carried_out[rows, head(h)] = carried.astype(BF16)
            out = diag[rows, head(h)] + carried
            gate = proj[rows, head(h)].astype(F32)
            sigmoid = 1.0 / (1.0 + jnp.exp(-gate))
            silu = gate * sigmoid
            silu_out[rows, head(h)] = silu
            gated_out[rows, head(h)] = out * silu
            slope_out[rows, head(h)] = out * sigmoid * (1.0 + gate * (1.0 - sigmoid))
        base = base + r[block - 1 : block, :]
        gated = gated_out[rows, :]
        sums_out[:, rows] = dot(ones, gated * gated, (1, 1), EXACT)


def token_sums(local, gain, gated, squares, sums_out):
    ones = jnp.ones((8, local.shape[1]), F32)
    cross = dot(ones, gain[...] * local[...] * gated[...], (1, 1), EXACT)
    upper = lax.broadcasted_iota(jnp.int32, cross.shape, 0) < 4
    sums_out[...] = jnp.where(upper, squares[...], cross)


def backward_gate(heads, block, total_width, local, gain, gated, silu, slope, act, run, *refs):
    parts = refs[:-5]
    dgate_out, cot_out, grown_out, blocks_out, own_out = refs[-5:]
    length = local.shape[0]
    width = heads * HEAD_DIM
    pick = lax.broadcasted_iota(jnp.int32, (8, LANES), 0)
    own = [jnp.zeros((HEAD_DIM, STATE), F32) for _ in range(heads)]
    base = jnp.zeros((1, LANES), F32)
    for k in range(length // block):
        rows = slice(k * block, (k + 1) * block)
        sums = parts[0][:, rows]
        for part in parts[1:]:
            sums = sums + part[:, rows]
        square = dot(sums, (pick == 0).astype(F32), (0, 0), EXACT) / total_width
        cross = dot(sums, (pick == 4).astype(F32), (0, 0), EXACT) / total_width
        inverse = lax.rsqrt(square + EPSILON)
        cross = cross * (inverse * inverse * inverse)
        r = run[rows, :]
        grow = jnp.exp(r)
        reach = jnp.exp(base)
        c_rows = act[rows, width + STATE :]
        for h in range(heads):
            at = k * heads + h
            d_gated = inverse * (gain[:, head(h)] * local[rows, head(h)]) - gated[rows, head(h)] * cross
            dgate_out[rows, head(h)] = (d_gated * slope[rows, head(h)]).astype(BF16)
            cot = d_gated * silu[rows, head(h)]
            cot_out[rows, head(h)] = cot.astype(BF16)
            grown = (grow[:, h : h + 1] * cot).astype(BF16)
            grown_out[rows, head(h)] = grown
            entering = dot(grown, c_rows, (0, 0))
            blocks_out[at * HEAD_DIM : (at + 1) * HEAD_DIM, :] = entering
            own[h] = own[h] + reach[:, h : h + 1] * entering
        base = base + r[block - 1 : block, :]
    for h in range(heads):
        own_out[head(h), :] = own[h]


def backward_local(
    heads, block, cot, grown, act, scaled, decays, table, states, carried, u_out, dbc_out, decay_out
):
    length = cot.shape[0]
    width = heads * HEAD_DIM
    before = triangle(block, lambda i, j: i > j)
    upper = triangle(block, lambda i, j: i <= j).astype(BF16)
    lane = lax.broadcasted_iota(jnp.int32, (block, LANES), 1)
    for k in range(length // block):
        rows = slice(k * block, (k + 1) * block)
        b_rows = act[rows, width : width + STATE]
        c_rows = act[rows, width + STATE :]
        d_brows = jnp.zeros((block, STATE), F32)
        d_crows = jnp.zeros((block, STATE), F32)
        decay = jnp.zeros((block, LANES), F32)
        for h in range(heads):
            at = k * heads + h
            g = cot[rows, head(h)]
            weights = table[rows, head(h)]
            inner = dot(g, scaled[rows, head(h)], (1, 1))
            pairs = (decays[rows, head(h)].astype(F32) * inner).astype(BF16)
            mixed = (weights.astype(F32) * inner).astype(BF16)
            d_crows = d_crows + dot(pairs, b_rows)
            d_crows = d_crows + dot(grown[rows, head(h)], states[at * HEAD_DIM : (at + 1) * HEAD_DIM, :])
            d_brows = d_brows + dot(pairs, c_rows, (0, 0))
            u_out[rows, head(h)] = dot(weights, g, (0, 0))
            through = (g.astype(F32) * carried[rows, head(h)].astype(F32)).astype(BF16)
            spread = jnp.where(before, dot(upper, mixed), 0.0) + dot(upper, through)
            decay = jnp.where(lane == h, jnp.sum(spread, axis=1, keepdims=True), decay)
        dbc_out[rows, :STATE] = d_brows
        dbc_out[rows, STATE:] = d_crows
        decay_out[rows, :] = decay


def backward_carried(
    heads, block, dgate, act, scaled, slope, step, run, sig, rate, kern, states, blocks, u, dbc, decay, weights,
    *refs,
):
    received = refs[:-4]
    cat_out, end_out, tail_out, scr = refs[-4:]
    length = dgate.shape[0]
    width = heads * HEAD_DIM
    conv_width = width + 2 * STATE
    strict = triangle(block, lambda i, j: i > j).astype(BF16)
    lane = lax.broadcasted_iota(jnp.int32, (block, LANES), 1)
    scr[0:PAD, :] = jnp.zeros((PAD, conv_width), F32)
    scr[PAD + length :, :] = jnp.zeros((PAD, conv_width), F32)
    cat_out[:, :width] = dgate[...]
    leaving = []
    for h in range(heads):
        total = jnp.zeros((HEAD_DIM, STATE), F32)
        for i, part in enumerate(received):
            total = total + weights[i * heads + h : i * heads + h + 1, :] * part[head(h), :]
        leaving.append(total)
    for k in reversed(range(length // block)):
        rows = slice(k * block, (k + 1) * block)
        into = slice(PAD + k * block, PAD + (k + 1) * block)
        r = run[rows, :]
        last = r[block - 1 : block, :]
        shrink = jnp.exp(last - r)
        whole = jnp.exp(last)
        b_rows = act[rows, width : width + STATE]
        d_brows = dbc[rows, :STATE]
        d_step = jnp.zeros((block, LANES), F32)
        for h in range(heads):
            at = k * heads + h
            here = slice(at * HEAD_DIM, (at + 1) * HEAD_DIM)
            cot_state = leaving[h].astype(BF16)
            past = shrink[:, h : h + 1] * dot(b_rows, cot_state, (1, 1))
            total = u[rows, head(h)] + past
            moved = scaled[rows, head(h)].astype(F32)
            d_brows = d_brows + dot((shrink[:, h : h + 1] * moved).astype(BF16), cot_state)
            kept = whole[:, h : h + 1] * leaving[h]
            constant = jnp.sum(
                jnp.sum(kept * states[here, :].astype(F32), axis=1, keepdims=True), axis=0, keepdims=True
            )
            spread = dot(strict, (moved * past).astype(BF16))
            d_decay = jnp.sum(spread, axis=1, keepdims=True) + constant + decay[rows, h : h + 1]
            direct = jnp.sum(act[rows, head(h)].astype(F32) * total, axis=1, keepdims=True)
            d_step = jnp.where(lane == h, direct - rate[:, h : h + 1] * d_decay, d_step)
            scr[into, head(h)] = step[rows, h : h + 1] * total * slope[rows, head(h)]
            leaving[h] = kept + blocks[here, :]
        scr[into, width : width + STATE] = d_brows * slope[rows, width : width + STATE]
        scr[into, width + STATE :] = dbc[rows, STATE:] * slope[rows, width + STATE :]
        cat_out[rows, width + conv_width :] = (d_step * sig[rows, :]).astype(BF16)
        value = kern[CONV - 1 : CONV, :] * scr[into, :]
        for j in range(1, CONV):
            value = value + kern[CONV - 1 - j : CONV - j, :] * scr[into.start + j : into.stop + j, :]
        cat_out[rows, width : width + conv_width] = value.astype(BF16)
        if k == length // block - 1:
            end_out[...] = value[block - PAD :, :]
    value = kern[CONV - 1 : CONV, :] * scr[0:PAD, :]
    for j in range(1, CONV):
        value = value + kern[CONV - 1 - j : CONV - j, :] * scr[j : PAD + j, :]
    tail_out[...] = value


def turned(value, axis, by):
    length = lax.axis_size(axis)
    return lax.ppermute(value, axis, [(i, (i + by) % length) for i in range(length)])


def paired(value, by):
    length = lax.axis_size("tp")
    return lax.ppermute(value, "tp", [(i, i ^ by) for i in range(length)])


def shifted(value, axis, by):
    length = lax.axis_size(axis)
    pairs = [(i, i + by) for i in range(length) if 0 <= i + by < length]
    return lax.ppermute(value, axis, pairs)


def after(value, token):
    columns = value.shape[1] if value.shape[1] <= token.shape[1] else 1
    return value + (token[:1, :columns] * 0).astype(value.dtype)


def halves(held):
    return ((0, held // 2), (held // 2, held - held // 2))


def ring_gather(parts, consume, result):
    chips = lax.axis_size("tp") // 2
    index = lax.axis_index("tp")
    chip, core = index // 2, index % 2
    arrived = []
    for step in range(chips):
        beside = [paired(part, 1) for part in parts]
        source = (chip - step) % chips
        owners = (source * 2 + core, source * 2 + 1 - core)
        if step < chips - 1:
            following = [turned(part, "tp", 2) for part in parts]
            result = consume(result, parts + beside, owners, None)
            parts = following
            arrived.append(parts)
        else:
            for i in range(len(parts)):
                result = consume(result, [parts[i], beside[i]], owners, i)
    return result, arrived


def multiply_into(weight, over, held, dtype):
    cuts = halves(held)

    def consume(result, rows, owners, only):
        product = dot(jnp.concatenate(rows, axis=0), weight, over).astype(dtype)
        at, size = (0, held) if only is None else cuts[only]
        for i, owner in enumerate(owners):
            piece = product[i * size : (i + 1) * size]
            result = lax.dynamic_update_slice(result, piece, (owner * held + at, 0))
        return result

    return consume


def product_rows(rows, weight, beside_out, mine_out):
    product = dot(rows[...], weight[...], (1, 1)).astype(BF16)
    count = beside_out.shape[0]
    beside_out[...] = product[:count]
    mine_out[...] = product[count:]


def multiply_rows(rows, weight):
    depth, inner = weight.shape
    block = math.gcd(depth, 512)
    count = rows.shape[0] // 2
    out = pl.BlockSpec((count, block), lambda i: (0, i))
    return pl.pallas_call(
        product_rows,
        grid=(depth // block,),
        in_specs=[pl.BlockSpec(rows.shape, lambda i: (0, 0)), pl.BlockSpec((block, inner), lambda i: (i, 0))],
        out_specs=[out, out],
        out_shape=[shape(count, depth, dtype=BF16)] * 2,
        name="product_rows",
        compiler_params=pltpu.CompilerParams(vmem_limit_bytes=VMEM_LIMIT),
        cost_estimate=COST,
    )(rows, weight)


def ring_scatter(cat_parts, weight, held):
    chips = lax.axis_size("tp") // 2
    index = lax.axis_index("tp")
    chip, core = index // 2, index % 2
    inner = weight.shape[1]
    shares = []
    totals = []
    for cat, (at, size) in zip(cat_parts, halves(held)):
        rows = [
            lax.dynamic_slice(cat, ((((chip - 1 - step) % chips) * 2 + side) * held + at, 0), (size, inner))
            for side in (1 - core, core)
            for step in range(chips)
        ]
        other, own = multiply_rows(jnp.concatenate(rows, axis=0), weight)
        beside = paired(other, 1)
        shares.append((own, beside))
        totals.append((own[:size].astype(F32) + beside[:size].astype(F32)).astype(BF16))
    started = list(totals)
    for step in range(1, chips):
        for i, (at, size) in enumerate(halves(held)):
            own, beside = [share[step * size : (step + 1) * size].astype(F32) for share in shares[i]]
            if step == 1 and i == 0:
                own = after(own, started[1])
            totals[i] = (own + beside + turned(totals[i], "tp", 2).astype(F32)).astype(BF16)
    return jnp.concatenate(totals, axis=0)


def shape(*dims, dtype=F32):
    return jax.ShapeDtypeStruct(dims, dtype)


def body(
    normed_rows, out_grad, inner_weight, state_weight, step_weight, conv_inner, conv_state,
    step_bias, decay_log, norm_gain, out_weight,
):
    width = inner_weight.shape[2]
    heads = step_bias.shape[0]
    members = lax.axis_size("tp")
    shards = lax.axis_size("ctx")
    mine = lax.axis_index("ctx")
    length = normed_rows.shape[0] * members
    block = math.gcd(length, 128)
    count = length // block
    conv_width = width + 2 * STATE

    weight_cat = jnp.concatenate(
        [inner_weight[0], inner_weight[1], state_weight, jnp.pad(step_weight, ((0, 0), (0, LANES - heads)))],
        axis=1,
    )
    kern = jnp.concatenate([conv_inner, conv_state], axis=1)
    bias = jnp.pad(step_bias, (0, LANES - heads))[None]
    rate = jnp.pad(jnp.exp(decay_log), (0, LANES - heads))[None]
    gain = norm_gain[None]

    held, depth = normed_rows.shape
    cuts = halves(held)
    proj, rows_in = ring_gather(
        [normed_rows[at : at + size] for at, size in cuts],
        multiply_into(weight_cat, (1, 0), held, BF16),
        jnp.zeros((length, weight_cat.shape[1]), BF16),
    )
    local, grads_in = ring_gather(
        [after(out_grad[at : at + size], rows_in[-1][i]) for i, (at, size) in enumerate(cuts)],
        multiply_into(out_weight, (1, 1), held, F32),
        jnp.zeros((length, width), F32),
    )

    tail = shifted(proj[length - PAD :, width : width + conv_width], "ctx", 1)
    act, scaled, slope, step, run, sig, decays, table, diag, states, own = pl.pallas_call(
        partial(forward_local, heads, block),
        out_shape=[
            shape(length, conv_width, dtype=BF16),
            shape(length, width, dtype=BF16),
            shape(length, conv_width),
            shape(length, LANES),
            shape(length, LANES),
            shape(length, LANES),
            shape(length, heads * block, dtype=BF16),
            shape(length, heads * block, dtype=BF16),
            shape(length, width),
            shape(count * heads * HEAD_DIM, STATE),
            shape(heads * HEAD_DIM, STATE),
        ],
        scratch_shapes=[pltpu.VMEM((PAD + length, conv_width), F32)],
        name="forward_local",
        **PARAMS,
    )(proj, tail, kern, bias, rate)

    ends = run.reshape(count, block, LANES)[:, block - 1, :heads]
    total_log = jnp.sum(ends, axis=0)
    message = jnp.concatenate([own, jnp.broadcast_to(jnp.pad(total_log, (0, LANES - heads)), (8, LANES))], axis=0)
    second = grads_in[min(1, len(grads_in) - 1)]
    message = after(message, second[0])
    received = [turned(message, "ctx", by) for by in range(1, shards)]
    logs = [part[heads * HEAD_DIM, :heads] for part in received]
    entering_weights = []
    between = jnp.zeros((heads,), F32)
    for by in range(1, shards):
        entering_weights.append(jnp.where(mine >= by, jnp.exp(between), 0.0))
        between = between + jnp.where(mine >= by, logs[by - 1], 0.0)
    leaving_weights = []
    between = jnp.zeros((heads,), F32)
    for by in range(1, shards):
        leaving_weights.append(jnp.where(mine + by < shards, jnp.exp(between), 0.0))
        between = between + jnp.where(mine + by < shards, logs[shards - by - 1], 0.0)

    def spread(parts):
        flat = jnp.concatenate(parts)
        return jnp.broadcast_to(flat[:, None], (flat.shape[0], LANES))

    gated, silu, gate_slope, carried, full_states, squares = pl.pallas_call(
        partial(forward_carried, heads, block),
        out_shape=[
            shape(length, width),
            shape(length, width),
            shape(length, width),
            shape(length, width, dtype=BF16),
            shape(count * heads * HEAD_DIM, STATE, dtype=BF16),
            shape(8, length),
        ],
        name="forward_carried",
        **PARAMS,
    )(proj, act, run, diag, states, after(spread(entering_weights), second[1]), *received)

    sums = pl.pallas_call(token_sums, out_shape=shape(8, length), name="token_sums", **PARAMS)(
        local, gain, gated, squares
    )

    sums = sums + paired(sums, 1)
    parts = [sums] + [turned(sums, "tp", by) for by in range(2, members, 2)]

    dgate, cot, grown, blocks, own_cot = pl.pallas_call(
        partial(backward_gate, heads, block, width * members),
        out_shape=[
            shape(length, width, dtype=BF16),
            shape(length, width, dtype=BF16),
            shape(length, width, dtype=BF16),
            shape(count * heads * HEAD_DIM, STATE),
            shape(heads * HEAD_DIM, STATE),
        ],
        name="backward_gate",
        **PARAMS,
    )(local, gain, gated, silu, gate_slope, act, run, *parts)

    returned = [turned(own_cot, "ctx", -by) for by in range(1, shards)]

    u, dbc, decay = pl.pallas_call(
        partial(backward_local, heads, block),
        out_shape=[shape(length, width), shape(length, 2 * STATE), shape(length, LANES)],
        name="backward_local",
        **PARAMS,
    )(cot, grown, act, scaled, decays, table, full_states, carried)

    cat, end, tail_cot = pl.pallas_call(
        partial(backward_carried, heads, block),
        out_shape=[
            shape(length, width + conv_width + LANES, dtype=BF16),
            shape(PAD, conv_width),
            shape(PAD, conv_width),
        ],
        scratch_shapes=[pltpu.VMEM((length + 2 * PAD, conv_width), F32)],
        name="backward_carried",
        **PARAMS,
    )(
        dgate, act, scaled, slope, step, run, sig, rate, kern, full_states, blocks, u, dbc, decay,
        spread(leaving_weights), *returned,
    )

    incoming = shifted(tail_cot, "ctx", -1)
    whole = lax.dynamic_update_slice(cat, (end + incoming).astype(BF16), (length - PAD, width))
    return ring_scatter((cat, whole), weight_cat, held)


def solution(mesh):
    placed = (
        P(("ctx", "tp"), None),
        P(("ctx", "tp"), None),
        P(None, None, "tp"),
        P(),
        P(None, "tp"),
        P(None, "tp"),
        P(),
        P("tp"),
        P("tp"),
        P("tp"),
        P("tp", None),
    )
    return jax.shard_map(
        body, mesh=mesh, in_specs=placed, out_specs=P(("ctx", "tp"), None), check_vma=False
    )
```

```python
import math
from functools import partial

import jax
import jax.numpy as jnp
from jax import lax
from jax.experimental import pallas as pl
from jax.experimental.pallas import tpu as pltpu
from jax.sharding import PartitionSpec as P

HEAD_DIM = 128
STATE = 128
CONV = 4
LANES = 128
PAD = 8
EPSILON = 1e-05
EXACT = lax.Precision.HIGHEST
F32 = jnp.float32
BF16 = jnp.bfloat16
COST = pl.CostEstimate(flops=1000, bytes_accessed=1000, transcendentals=0)
VMEM_LIMIT = 16 * 1024 * 1024
PARAMS = dict(
    compiler_params=pltpu.CompilerParams(vmem_limit_bytes=16 * 1024 * 1024), cost_estimate=COST
)


def dot(a, b, over=(1, 0), precision=None):
    return lax.dot_general(
        a, b, (((over[0],), (over[1],)), ((), ())), precision=precision, preferred_element_type=F32
    )


def triangle(size, keep):
    rows = lax.broadcasted_iota(jnp.int32, (size, size), 0)
    columns = lax.broadcasted_iota(jnp.int32, (size, size), 1)
    return keep(rows, columns)


def head(h):
    return slice(h * HEAD_DIM, (h + 1) * HEAD_DIM)


def columns(ref, *widths):
    views = []
    first = 0
    for size in widths:
        views.append(ref.at[:, first : first + size])
        first = first + size
    return views


def forward_local(
    heads, block, proj, tail, kern, bias, rate,
    saved_out, factors_out, diag_out, states_out, own_out, ext,
):
    length = proj.shape[0]
    width = heads * HEAD_DIM
    conv_width = width + 2 * STATE
    act_out, scaled_out, decay_out, table_out = columns(saved_out, conv_width, width, width, width)
    slope_out, step_out, run_out, sig_out = columns(factors_out, conv_width, LANES, LANES, LANES)
    ext[0:PAD, :] = tail[...].astype(F32)
    ext[PAD:, :] = proj[:, width : width + conv_width].astype(F32)
    causal = triangle(block, lambda i, j: i >= j)
    lower = causal.astype(F32)
    state = [jnp.zeros((HEAD_DIM, STATE), F32) for _ in range(heads)]
    for k in range(length // block):
        rows = slice(k * block, (k + 1) * block)
        first = k * block + PAD - (CONV - 1)
        value = kern[0:1, :] * ext[first : first + block, :]
        for j in range(1, CONV):
            value = value + kern[j : j + 1, :] * ext[first + j : first + j + block, :]
        sigmoid = 1.0 / (1.0 + jnp.exp(-value))
        act = value * sigmoid
        act_out[rows, :] = act.astype(BF16)
        slope_out[rows, :] = sigmoid * (1.0 + value * (1.0 - sigmoid))
        raw = proj[rows, width + conv_width :].astype(F32) + bias[...]
        grown = jnp.exp(-jnp.abs(raw))
        step = jnp.maximum(raw, 0.0) + jnp.log1p(grown)
        step_out[rows, :] = step
        sig_out[rows, :] = jnp.where(raw >= 0.0, 1.0, grown) / (1.0 + grown)
        run = dot(lower, -step * rate[...], precision=EXACT)
        run_out[rows, :] = run
        run_t = run.T
        b_rows = act[:, width : width + STATE]
        c_rows = act[:, width + STATE :]
        scores = dot(c_rows, b_rows, (1, 1), EXACT)
        for h in range(heads):
            at = k * heads + h
            col = run[:, h : h + 1]
            decay = jnp.where(causal, jnp.exp(jnp.minimum(col - run_t[h : h + 1, :], 0.0)), 0.0)
            table = decay * scores
            scaled = act[:, head(h)] * step[:, h : h + 1]
            scaled_out[rows, head(h)] = scaled.astype(BF16)
            decay_out[rows, head(h)] = decay.astype(BF16)
            table_out[rows, head(h)] = table.astype(BF16)
            diag_out[rows, head(h)] = dot(table, scaled, precision=EXACT)
            states_out[at * HEAD_DIM : (at + 1) * HEAD_DIM, :] = state[h]
            last = run[block - 1 : block, h : h + 1]
            state[h] = jnp.exp(last) * state[h] + dot(
                jnp.exp(last - col) * scaled, b_rows, (0, 0), EXACT
            )
    for h in range(heads):
        own_out[head(h), :] = state[h]


def forward_carried(
    heads, block, proj, saved, factors, diag, states, weights, *refs,
):
    received = refs[:-3]
    gates_out, sent_out, sums_out = refs[-3:]
    length = proj.shape[0]
    width = heads * HEAD_DIM
    conv_width = width + 2 * STATE
    (act,) = columns(saved, conv_width)
    _, _, run = columns(factors, conv_width, LANES, LANES)
    gated_out, silu_out, slope_out = columns(gates_out, width, width, width)
    carried_out, states_out = columns(sent_out, width, width)
    entering = []
    for h in range(heads):
        total = jnp.zeros((HEAD_DIM, STATE), F32)
        for i, part in enumerate(received):
            total = total + weights[i * heads + h : i * heads + h + 1, :] * part[head(h), :]
        entering.append(total)
    base = jnp.zeros((1, LANES), F32)
    ones = jnp.ones((8, width), F32)
    for k in range(length // block):
        rows = slice(k * block, (k + 1) * block)
        r = run[rows, :]
        grow = jnp.exp(r)
        reach = jnp.exp(base)
        c_rows = act[rows, width + STATE :].astype(F32)
        for h in range(heads):
            at = k * heads + h
            here = slice(at * HEAD_DIM, (at + 1) * HEAD_DIM)
            state = states[here, :] + reach[:, h : h + 1] * entering[h]
            states_out[rows, head(h)] = state.astype(BF16)
            carried = grow[:, h : h + 1] * dot(c_rows, state, (1, 1), EXACT)
            carried_out[rows, head(h)] = carried.astype(BF16)
            out = diag[rows, head(h)] + carried
            gate = proj[rows, head(h)].astype(F32)
            sigmoid = 1.0 / (1.0 + jnp.exp(-gate))
            silu = gate * sigmoid
            silu_out[rows, head(h)] = silu
            gated_out[rows, head(h)] = out * silu
            slope_out[rows, head(h)] = out * sigmoid * (1.0 + gate * (1.0 - sigmoid))
        base = base + r[block - 1 : block, :]
        gated = gated_out[rows, :]
        sums_out[:, rows] = dot(ones, gated * gated, (1, 1), EXACT)


def token_sums(local, gain, gates, squares, sums_out):
    (gated,) = columns(gates, local.shape[1])
    ones = jnp.ones((8, local.shape[1]), F32)
    cross = dot(ones, gain[...] * local[...] * gated[...], (1, 1), EXACT)
    upper = lax.broadcasted_iota(jnp.int32, cross.shape, 0) < 4
    sums_out[...] = jnp.where(upper, squares[...], cross)


def backward_gate(heads, block, total_width, local, gain, gates, saved, factors, *refs):
    parts = refs[:-3]
    cots_out, blocks_out, own_out = refs[-3:]
    length = local.shape[0]
    width = heads * HEAD_DIM
    conv_width = width + 2 * STATE
    gated, silu, slope = columns(gates, width, width, width)
    (act,) = columns(saved, conv_width)
    _, _, run = columns(factors, conv_width, LANES, LANES)
    dgate_out, cot_out, grown_out = columns(cots_out, width, width, width)
    pick = lax.broadcasted_iota(jnp.int32, (8, LANES), 0)
    own = [jnp.zeros((HEAD_DIM, STATE), F32) for _ in range(heads)]
    base = jnp.zeros((1, LANES), F32)
    for k in range(length // block):
        rows = slice(k * block, (k + 1) * block)
        sums = parts[0][:, rows]
        for part in parts[1:]:
            sums = sums + part[:, rows]
        square = dot(sums, (pick == 0).astype(F32), (0, 0), EXACT) / total_width
        cross = dot(sums, (pick == 4).astype(F32), (0, 0), EXACT) / total_width
        inverse = lax.rsqrt(square + EPSILON)
        cross = cross * (inverse * inverse * inverse)
        r = run[rows, :]
        grow = jnp.exp(r)
        reach = jnp.exp(base)
        c_rows = act[rows, width + STATE :]
        for h in range(heads):
            at = k * heads + h
            d_gated = inverse * (gain[:, head(h)] * local[rows, head(h)]) - gated[rows, head(h)] * cross
            dgate_out[rows, head(h)] = (d_gated * slope[rows, head(h)]).astype(BF16)
            cot = d_gated * silu[rows, head(h)]
            cot_out[rows, head(h)] = cot.astype(BF16)
            grown = (grow[:, h : h + 1] * cot).astype(BF16)
            grown_out[rows, head(h)] = grown
            entering = dot(grown, c_rows, (0, 0))
            blocks_out[at * HEAD_DIM : (at + 1) * HEAD_DIM, :] = entering
            own[h] = own[h] + reach[:, h : h + 1] * entering
        base = base + r[block - 1 : block, :]
    for h in range(heads):
        own_out[head(h), :] = own[h]


def backward_local(heads, block, cots, saved, sent, near_out):
    length = cots.shape[0]
    width = heads * HEAD_DIM
    _, cot, grown = columns(cots, width, width, width)
    act, scaled, decays, table = columns(saved, width + 2 * STATE, width, width, width)
    carried, states = columns(sent, width, width)
    u_out, dbc_out, decay_out = columns(near_out, width, 2 * STATE, LANES)
    before = triangle(block, lambda i, j: i > j)
    upper = triangle(block, lambda i, j: i <= j).astype(BF16)
    lane = lax.broadcasted_iota(jnp.int32, (block, LANES), 1)
    for k in range(length // block):
        rows = slice(k * block, (k + 1) * block)
        b_rows = act[rows, width : width + STATE]
        c_rows = act[rows, width + STATE :]
        d_brows = jnp.zeros((block, STATE), F32)
        d_crows = jnp.zeros((block, STATE), F32)
        decay = jnp.zeros((block, LANES), F32)
        for h in range(heads):
            g = cot[rows, head(h)]
            weights = table[rows, head(h)]
            inner = dot(g, scaled[rows, head(h)], (1, 1))
            pairs = (decays[rows, head(h)].astype(F32) * inner).astype(BF16)
            mixed = (weights.astype(F32) * inner).astype(BF16)
            d_crows = d_crows + dot(pairs, b_rows)
            d_crows = d_crows + dot(grown[rows, head(h)], states[rows, head(h)])
            d_brows = d_brows + dot(pairs, c_rows, (0, 0))
            u_out[rows, head(h)] = dot(weights, g, (0, 0))
            through = (g.astype(F32) * carried[rows, head(h)].astype(F32)).astype(BF16)
            spread = jnp.where(before, dot(upper, mixed), 0.0) + dot(upper, through)
            decay = jnp.where(lane == h, jnp.sum(spread, axis=1, keepdims=True), decay)
        dbc_out[rows, :STATE] = d_brows
        dbc_out[rows, STATE:] = d_crows
        decay_out[rows, :] = decay


def backward_carried(
    heads, block, cots, saved, factors, rate, kern, sent, blocks, near, weights, *refs,
):
    received = refs[:-4]
    cat_out, end_out, tail_out, scr = refs[-4:]
    length = cots.shape[0]
    width = heads * HEAD_DIM
    conv_width = width + 2 * STATE
    (dgate,) = columns(cots, width)
    act, scaled = columns(saved, conv_width, width)
    slope, step, run, sig = columns(factors, conv_width, LANES, LANES, LANES)
    _, states = columns(sent, width, width)
    u, dbc, decay = columns(near, width, 2 * STATE, LANES)
    strict = triangle(block, lambda i, j: i > j).astype(BF16)
    lane = lax.broadcasted_iota(jnp.int32, (block, LANES), 1)
    scr[0:PAD, :] = jnp.zeros((PAD, conv_width), F32)
    scr[PAD + length :, :] = jnp.zeros((PAD, conv_width), F32)
    cat_out[:, :width] = dgate[...]
    leaving = []
    for h in range(heads):
        total = jnp.zeros((HEAD_DIM, STATE), F32)
        for i, part in enumerate(received):
            total = total + weights[i * heads + h : i * heads + h + 1, :] * part[head(h), :]
        leaving.append(total)
    for k in reversed(range(length // block)):
        rows = slice(k * block, (k + 1) * block)
        into = slice(PAD + k * block, PAD + (k + 1) * block)
        r = run[rows, :]
        last = r[block - 1 : block, :]
        shrink = jnp.exp(last - r)
        whole = jnp.exp(last)
        b_rows = act[rows, width : width + STATE]
        d_brows = dbc[rows, :STATE]
        d_step = jnp.zeros((block, LANES), F32)
        for h in range(heads):
            at = k * heads + h
            here = slice(at * HEAD_DIM, (at + 1) * HEAD_DIM)
            cot_state = leaving[h].astype(BF16)
            past = shrink[:, h : h + 1] * dot(b_rows, cot_state, (1, 1))
            total = u[rows, head(h)] + past
            moved = scaled[rows, head(h)].astype(F32)
            d_brows = d_brows + dot((shrink[:, h : h + 1] * moved).astype(BF16), cot_state)
            kept = whole[:, h : h + 1] * leaving[h]
            constant = jnp.sum(
                jnp.sum(kept * states[rows, head(h)].astype(F32), axis=1, keepdims=True), axis=0, keepdims=True
            )
            spread = dot(strict, (moved * past).astype(BF16))
            d_decay = jnp.sum(spread, axis=1, keepdims=True) + constant + decay[rows, h : h + 1]
            direct = jnp.sum(act[rows, head(h)].astype(F32) * total, axis=1, keepdims=True)
            d_step = jnp.where(lane == h, direct - rate[:, h : h + 1] * d_decay, d_step)
            scr[into, head(h)] = step[rows, h : h + 1] * total * slope[rows, head(h)]
            leaving[h] = kept + blocks[here, :]
        scr[into, width : width + STATE] = d_brows * slope[rows, width : width + STATE]
        scr[into, width + STATE :] = dbc[rows, STATE:] * slope[rows, width + STATE :]
        cat_out[rows, width + conv_width :] = (d_step * sig[rows, :]).astype(BF16)
        value = kern[CONV - 1 : CONV, :] * scr[into, :]
        for j in range(1, CONV):
            value = value + kern[CONV - 1 - j : CONV - j, :] * scr[into.start + j : into.stop + j, :]
        cat_out[rows, width : width + conv_width] = value.astype(BF16)
        if k == length // block - 1:
            end_out[...] = value[block - PAD :, :]
    value = kern[CONV - 1 : CONV, :] * scr[0:PAD, :]
    for j in range(1, CONV):
        value = value + kern[CONV - 1 - j : CONV - j, :] * scr[j : PAD + j, :]
    tail_out[...] = value


def turned(value, axis, by):
    length = lax.axis_size(axis)
    return lax.ppermute(value, axis, [(i, (i + by) % length) for i in range(length)])


def paired(value, by):
    length = lax.axis_size("tp")
    return lax.ppermute(value, "tp", [(i, i ^ by) for i in range(length)])


def shifted(value, axis, by):
    length = lax.axis_size(axis)
    pairs = [(i, i + by) for i in range(length) if 0 <= i + by < length]
    return lax.ppermute(value, axis, pairs)


def after(value, token):
    columns = value.shape[1] if value.shape[1] <= token.shape[1] else 1
    return value + (token[:1, :columns] * 0).astype(value.dtype)


def halves(held):
    return ((0, held // 2), (held // 2, held - held // 2))


def ring_gather(parts, consume, result):
    chips = lax.axis_size("tp") // 2
    index = lax.axis_index("tp")
    chip, core = index // 2, index % 2
    arrived = []
    for step in range(chips):
        beside = [paired(part, 1) for part in parts]
        source = (chip - step) % chips
        owners = (source * 2 + core, source * 2 + 1 - core)
        if step < chips - 1:
            following = [turned(part, "tp", 2) for part in parts]
            result = consume(result, parts + beside, owners, None)
            parts = following
            arrived.append(parts)
        else:
            for i in range(len(parts)):
                result = consume(result, [parts[i], beside[i]], owners, i)
    return result, arrived


def multiply_into(weight, over, held, dtype):
    cuts = halves(held)

    def consume(result, rows, owners, only):
        product = dot(jnp.concatenate(rows, axis=0), weight, over).astype(dtype)
        at, size = (0, held) if only is None else cuts[only]
        for i, owner in enumerate(owners):
            piece = product[i * size : (i + 1) * size]
            result = lax.dynamic_update_slice(result, piece, (owner * held + at, 0))
        return result

    return consume


def product_rows(rows, weight, beside_out, mine_out):
    product = dot(rows[...], weight[...], (1, 1)).astype(BF16)
    count = beside_out.shape[0]
    beside_out[...] = product[:count]
    mine_out[...] = product[count:]


def multiply_rows(rows, weight):
    depth, inner = weight.shape
    block = math.gcd(depth, 512)
    count = rows.shape[0] // 2
    out = pl.BlockSpec((count, block), lambda i: (0, i))
    return pl.pallas_call(
        product_rows,
        grid=(depth // block,),
        in_specs=[pl.BlockSpec(rows.shape, lambda i: (0, 0)), pl.BlockSpec((block, inner), lambda i: (i, 0))],
        out_specs=[out, out],
        out_shape=[shape(count, depth, dtype=BF16)] * 2,
        name="product_rows",
        compiler_params=pltpu.CompilerParams(vmem_limit_bytes=VMEM_LIMIT),
        cost_estimate=COST,
    )(rows, weight)


def ring_scatter(cat_parts, weight, held):
    chips = lax.axis_size("tp") // 2
    index = lax.axis_index("tp")
    chip, core = index // 2, index % 2
    inner = weight.shape[1]
    shares = []
    totals = []
    for cat, (at, size) in zip(cat_parts, halves(held)):
        rows = [
            lax.dynamic_slice(cat, ((((chip - 1 - step) % chips) * 2 + side) * held + at, 0), (size, inner))
            for side in (1 - core, core)
            for step in range(chips)
        ]
        other, own = multiply_rows(jnp.concatenate(rows, axis=0), weight)
        beside = paired(other, 1)
        shares.append((own, beside))
        totals.append((own[:size].astype(F32) + beside[:size].astype(F32)).astype(BF16))
    started = list(totals)
    for step in range(1, chips):
        for i, (at, size) in enumerate(halves(held)):
            own, beside = [share[step * size : (step + 1) * size].astype(F32) for share in shares[i]]
            if step == 1 and i == 0:
                own = after(own, started[1])
            totals[i] = (own + beside + turned(totals[i], "tp", 2).astype(F32)).astype(BF16)
    return jnp.concatenate(totals, axis=0)


def shape(*dims, dtype=F32):
    return jax.ShapeDtypeStruct(dims, dtype)


def body(
    normed_rows, out_grad, inner_weight, state_weight, step_weight, conv_inner, conv_state,
    step_bias, decay_log, norm_gain, out_weight,
):
    width = inner_weight.shape[2]
    heads = step_bias.shape[0]
    members = lax.axis_size("tp")
    shards = lax.axis_size("ctx")
    mine = lax.axis_index("ctx")
    length = normed_rows.shape[0] * members
    block = math.gcd(length, 128)
    count = length // block
    conv_width = width + 2 * STATE

    weight_cat = jnp.concatenate(
        [inner_weight[0], inner_weight[1], state_weight, jnp.pad(step_weight, ((0, 0), (0, LANES - heads)))],
        axis=1,
    )
    kern = jnp.concatenate([conv_inner, conv_state], axis=1)
    bias = jnp.pad(step_bias, (0, LANES - heads))[None]
    rate = jnp.pad(jnp.exp(decay_log), (0, LANES - heads))[None]
    gain = norm_gain[None]

    held, depth = normed_rows.shape
    cuts = halves(held)
    proj, rows_in = ring_gather(
        [normed_rows[at : at + size] for at, size in cuts],
        multiply_into(weight_cat, (1, 0), held, BF16),
        jnp.zeros((length, weight_cat.shape[1]), BF16),
    )
    local, grads_in = ring_gather(
        [after(out_grad[at : at + size], rows_in[-1][i]) for i, (at, size) in enumerate(cuts)],
        multiply_into(out_weight, (1, 1), held, F32),
        jnp.zeros((length, width), F32),
    )

    tail = after(proj[length - PAD :, width : width + conv_width], grads_in[0][1])
    tail = after(shifted(tail, "ctx", 1), grads_in[0][0])
    saved, factors, diag, states, own = pl.pallas_call(
        partial(forward_local, heads, block),
        out_shape=[
            shape(length, conv_width + 3 * width, dtype=BF16),
            shape(length, conv_width + 3 * LANES),
            shape(length, width),
            shape(count * heads * HEAD_DIM, STATE),
            shape(heads * HEAD_DIM, STATE),
        ],
        scratch_shapes=[pltpu.VMEM((PAD + length, conv_width), F32)],
        name="forward_local",
        **PARAMS,
    )(proj, tail, kern, bias, rate)

    run = factors[:, conv_width + LANES : conv_width + 2 * LANES]
    ends = run.reshape(count, block, LANES)[:, block - 1, :heads]
    total_log = jnp.sum(ends, axis=0)
    message = jnp.concatenate([own, jnp.broadcast_to(jnp.pad(total_log, (0, LANES - heads)), (8, LANES))], axis=0)
    second = grads_in[min(1, len(grads_in) - 1)]
    message = after(message, second[1])
    received = [turned(message, "ctx", by) for by in range(1, shards)]
    logs = [part[heads * HEAD_DIM, :heads] for part in received]
    entering_weights = []
    between = jnp.zeros((heads,), F32)
    for by in range(1, shards):
        entering_weights.append(jnp.where(mine >= by, jnp.exp(between), 0.0))
        between = between + jnp.where(mine >= by, logs[by - 1], 0.0)
    leaving_weights = []
    between = jnp.zeros((heads,), F32)
    for by in range(1, shards):
        leaving_weights.append(jnp.where(mine + by < shards, jnp.exp(between), 0.0))
        between = between + jnp.where(mine + by < shards, logs[shards - by - 1], 0.0)

    def spread(parts):
        flat = jnp.concatenate(parts)
        return jnp.broadcast_to(flat[:, None], (flat.shape[0], LANES))

    gates, sent, squares = pl.pallas_call(
        partial(forward_carried, heads, block),
        out_shape=[
            shape(length, 3 * width),
            shape(length, 2 * width, dtype=BF16),
            shape(8, length),
        ],
        name="forward_carried",
        **PARAMS,
    )(proj, saved, factors, diag, states, after(spread(entering_weights), second[0]), *received)

    sums = pl.pallas_call(token_sums, out_shape=shape(8, length), name="token_sums", **PARAMS)(
        local, gain, gates, squares
    )

    sums = sums + paired(sums, 1)
    parts = [sums] + [turned(sums, "tp", by) for by in range(2, members, 2)]

    cots, blocks, own_cot = pl.pallas_call(
        partial(backward_gate, heads, block, width * members),
        out_shape=[
            shape(length, 3 * width, dtype=BF16),
            shape(count * heads * HEAD_DIM, STATE),
            shape(heads * HEAD_DIM, STATE),
        ],
        name="backward_gate",
        **PARAMS,
    )(local, gain, gates, saved, factors, *parts)

    returned = [turned(own_cot, "ctx", -by) for by in range(1, shards)]

    near = pl.pallas_call(
        partial(backward_local, heads, block),
        out_shape=shape(length, width + 2 * STATE + LANES),
        name="backward_local",
        **PARAMS,
    )(cots, saved, sent)

    cat, end, tail_cot = pl.pallas_call(
        partial(backward_carried, heads, block),
        out_shape=[
            shape(length, width + conv_width + LANES, dtype=BF16),
            shape(PAD, conv_width),
            shape(PAD, conv_width),
        ],
        scratch_shapes=[pltpu.VMEM((length + 2 * PAD, conv_width), F32)],
        name="backward_carried",
        **PARAMS,
    )(
        cots, saved, factors, rate, kern, sent, blocks, near,
        spread(leaving_weights), *returned,
    )

    incoming = shifted(tail_cot, "ctx", -1)
    whole = lax.dynamic_update_slice(cat, (end + incoming).astype(BF16), (length - PAD, width))
    return ring_scatter((cat, whole), weight_cat, held)


def solution(mesh):
    placed = (
        P(("ctx", "tp"), None),
        P(("ctx", "tp"), None),
        P(None, None, "tp"),
        P(),
        P(None, "tp"),
        P(None, "tp"),
        P(),
        P("tp"),
        P("tp"),
        P("tp"),
        P("tp", None),
    )
    return jax.shard_map(
        body, mesh=mesh, in_specs=placed, out_specs=P(("ctx", "tp"), None), check_vma=False
    )
```

```python
import math
from functools import partial

import jax
import jax.numpy as jnp
from jax import lax
from jax.experimental import pallas as pl
from jax.experimental.pallas import tpu as pltpu
from jax.sharding import PartitionSpec as P

HEAD_DIM = 128
STATE = 128
CONV = 4
LANES = 128
PAD = 8
EPSILON = 1e-05
EXACT = lax.Precision.HIGHEST
F32 = jnp.float32
BF16 = jnp.bfloat16
COST = pl.CostEstimate(flops=1000, bytes_accessed=1000, transcendentals=0)
VMEM_LIMIT = 16 * 1024 * 1024
PARAMS = dict(
    compiler_params=pltpu.CompilerParams(vmem_limit_bytes=16 * 1024 * 1024), cost_estimate=COST
)


def dot(a, b, over=(1, 0), precision=None):
    return lax.dot_general(
        a, b, (((over[0],), (over[1],)), ((), ())), precision=precision, preferred_element_type=F32
    )


def triangle(size, keep):
    rows = lax.broadcasted_iota(jnp.int32, (size, size), 0)
    columns = lax.broadcasted_iota(jnp.int32, (size, size), 1)
    return keep(rows, columns)


def head(h):
    return slice(h * HEAD_DIM, (h + 1) * HEAD_DIM)


def columns(ref, *widths):
    views = []
    first = 0
    for size in widths:
        views.append(ref.at[:, first : first + size])
        first = first + size
    return views


def forward_local(
    heads, block, proj, tail, kern, bias, rate,
    saved_out, factors_out, diag_out, states_out, own_out, ext,
):
    length = proj.shape[0]
    width = heads * HEAD_DIM
    conv_width = width + 2 * STATE
    act_out, scaled_out, decay_out, table_out = columns(saved_out, conv_width, width, width, width)
    slope_out, step_out, run_out, sig_out = columns(factors_out, conv_width, LANES, LANES, LANES)
    ext[0:PAD, :] = tail[...].astype(F32)
    ext[PAD:, :] = proj[:, width : width + conv_width].astype(F32)
    causal = triangle(block, lambda i, j: i >= j)
    lower = causal.astype(F32)
    state = [jnp.zeros((HEAD_DIM, STATE), F32) for _ in range(heads)]
    for k in range(length // block):
        rows = slice(k * block, (k + 1) * block)
        first = k * block + PAD - (CONV - 1)
        value = kern[0:1, :] * ext[first : first + block, :]
        for j in range(1, CONV):
            value = value + kern[j : j + 1, :] * ext[first + j : first + j + block, :]
        sigmoid = 1.0 / (1.0 + jnp.exp(-value))
        act = value * sigmoid
        act_out[rows, :] = act.astype(BF16)
        slope_out[rows, :] = sigmoid * (1.0 + value * (1.0 - sigmoid))
        raw = proj[rows, width + conv_width :].astype(F32) + bias[...]
        grown = jnp.exp(-jnp.abs(raw))
        step = jnp.maximum(raw, 0.0) + jnp.log1p(grown)
        step_out[rows, :] = step
        sig_out[rows, :] = jnp.where(raw >= 0.0, 1.0, grown) / (1.0 + grown)
        run = dot(lower, -step * rate[...], precision=EXACT)
        run_out[rows, :] = run
        run_t = run.T
        b_rows = act[:, width : width + STATE]
        c_rows = act[:, width + STATE :]
        scores = dot(c_rows, b_rows, (1, 1), EXACT)
        for h in range(heads):
            at = k * heads + h
            col = run[:, h : h + 1]
            decay = jnp.where(causal, jnp.exp(jnp.minimum(col - run_t[h : h + 1, :], 0.0)), 0.0)
            table = decay * scores
            scaled = act[:, head(h)] * step[:, h : h + 1]
            scaled_out[rows, head(h)] = scaled.astype(BF16)
            decay_out[rows, head(h)] = decay.astype(BF16)
            table_out[rows, head(h)] = table.astype(BF16)
            diag_out[rows, head(h)] = dot(table, scaled, precision=EXACT)
            states_out[at * HEAD_DIM : (at + 1) * HEAD_DIM, :] = state[h]
            last = run[block - 1 : block, h : h + 1]
            state[h] = jnp.exp(last) * state[h] + dot(
                jnp.exp(last - col) * scaled, b_rows, (0, 0), EXACT
            )
    for h in range(heads):
        own_out[head(h), :] = state[h]


def forward_carried(
    heads, block, proj, saved, factors, diag, states, weights, *refs,
):
    received = refs[:-3]
    gates_out, sent_out, sums_out = refs[-3:]
    length = proj.shape[0]
    width = heads * HEAD_DIM
    conv_width = width + 2 * STATE
    (act,) = columns(saved, conv_width)
    _, _, run = columns(factors, conv_width, LANES, LANES)
    gated_out, silu_out, slope_out = columns(gates_out, width, width, width)
    carried_out, states_out = columns(sent_out, width, width)
    entering = []
    for h in range(heads):
        total = jnp.zeros((HEAD_DIM, STATE), F32)
        for i, part in enumerate(received):
            total = total + weights[i * heads + h : i * heads + h + 1, :] * part[head(h), :]
        entering.append(total)
    base = jnp.zeros((1, LANES), F32)
    ones = jnp.ones((8, width), F32)
    for k in range(length // block):
        rows = slice(k * block, (k + 1) * block)
        r = run[rows, :]
        grow = jnp.exp(r)
        reach = jnp.exp(base)
        c_rows = act[rows, width + STATE :].astype(F32)
        for h in range(heads):
            at = k * heads + h
            here = slice(at * HEAD_DIM, (at + 1) * HEAD_DIM)
            state = states[here, :] + reach[:, h : h + 1] * entering[h]
            states_out[rows, head(h)] = state.astype(BF16)
            carried = grow[:, h : h + 1] * dot(c_rows, state, (1, 1), EXACT)
            carried_out[rows, head(h)] = carried.astype(BF16)
            out = diag[rows, head(h)] + carried
            gate = proj[rows, head(h)].astype(F32)
            sigmoid = 1.0 / (1.0 + jnp.exp(-gate))
            silu = gate * sigmoid
            silu_out[rows, head(h)] = silu
            gated_out[rows, head(h)] = out * silu
            slope_out[rows, head(h)] = out * sigmoid * (1.0 + gate * (1.0 - sigmoid))
        base = base + r[block - 1 : block, :]
        gated = gated_out[rows, :]
        sums_out[:, rows] = dot(ones, gated * gated, (1, 1), EXACT)


def token_sums(local, gain, gates, squares, sums_out):
    (gated,) = columns(gates, local.shape[1])
    ones = jnp.ones((8, local.shape[1]), F32)
    cross = dot(ones, gain[...] * local[...] * gated[...], (1, 1), EXACT)
    upper = lax.broadcasted_iota(jnp.int32, cross.shape, 0) < 4
    sums_out[...] = jnp.where(upper, squares[...], cross)


def backward_gate(heads, block, total_width, local, gain, gates, saved, factors, *refs):
    parts = refs[:-3]
    cots_out, blocks_out, own_out = refs[-3:]
    length = local.shape[0]
    width = heads * HEAD_DIM
    conv_width = width + 2 * STATE
    gated, silu, slope = columns(gates, width, width, width)
    (act,) = columns(saved, conv_width)
    _, _, run = columns(factors, conv_width, LANES, LANES)
    dgate_out, cot_out, grown_out = columns(cots_out, width, width, width)
    pick = lax.broadcasted_iota(jnp.int32, (8, LANES), 0)
    own = [jnp.zeros((HEAD_DIM, STATE), F32) for _ in range(heads)]
    base = jnp.zeros((1, LANES), F32)
    for k in range(length // block):
        rows = slice(k * block, (k + 1) * block)
        sums = parts[0][:, rows]
        for part in parts[1:]:
            sums = sums + part[:, rows]
        square = dot(sums, (pick == 0).astype(F32), (0, 0), EXACT) / total_width
        cross = dot(sums, (pick == 4).astype(F32), (0, 0), EXACT) / total_width
        inverse = lax.rsqrt(square + EPSILON)
        cross = cross * (inverse * inverse * inverse)
        r = run[rows, :]
        grow = jnp.exp(r)
        reach = jnp.exp(base)
        c_rows = act[rows, width + STATE :]
        for h in range(heads):
            at = k * heads + h
            d_gated = inverse * (gain[:, head(h)] * local[rows, head(h)]) - gated[rows, head(h)] * cross
            dgate_out[rows, head(h)] = (d_gated * slope[rows, head(h)]).astype(BF16)
            cot = d_gated * silu[rows, head(h)]
            cot_out[rows, head(h)] = cot.astype(BF16)
            grown = (grow[:, h : h + 1] * cot).astype(BF16)
            grown_out[rows, head(h)] = grown
            entering = dot(grown, c_rows, (0, 0))
            blocks_out[at * HEAD_DIM : (at + 1) * HEAD_DIM, :] = entering
            own[h] = own[h] + reach[:, h : h + 1] * entering
        base = base + r[block - 1 : block, :]
    for h in range(heads):
        own_out[head(h), :] = own[h]


def backward_local(heads, block, cots, saved, sent, near_out):
    length = cots.shape[0]
    width = heads * HEAD_DIM
    _, cot, grown = columns(cots, width, width, width)
    act, scaled, decays, table = columns(saved, width + 2 * STATE, width, width, width)
    carried, states = columns(sent, width, width)
    u_out, dbc_out, decay_out = columns(near_out, width, 2 * STATE, LANES)
    before = triangle(block, lambda i, j: i > j)
    upper = triangle(block, lambda i, j: i <= j).astype(BF16)
    lane = lax.broadcasted_iota(jnp.int32, (block, LANES), 1)
    for k in range(length // block):
        rows = slice(k * block, (k + 1) * block)
        b_rows = act[rows, width : width + STATE]
        c_rows = act[rows, width + STATE :]
        d_brows = jnp.zeros((block, STATE), F32)
        d_crows = jnp.zeros((block, STATE), F32)
        decay = jnp.zeros((block, LANES), F32)
        for h in range(heads):
            g = cot[rows, head(h)]
            weights = table[rows, head(h)]
            inner = dot(g, scaled[rows, head(h)], (1, 1))
            pairs = (decays[rows, head(h)].astype(F32) * inner).astype(BF16)
            mixed = (weights.astype(F32) * inner).astype(BF16)
            d_crows = d_crows + dot(pairs, b_rows)
            d_crows = d_crows + dot(grown[rows, head(h)], states[rows, head(h)])
            d_brows = d_brows + dot(pairs, c_rows, (0, 0))
            u_out[rows, head(h)] = dot(weights, g, (0, 0))
            through = (g.astype(F32) * carried[rows, head(h)].astype(F32)).astype(BF16)
            spread = jnp.where(before, dot(upper, mixed), 0.0) + dot(upper, through)
            decay = jnp.where(lane == h, jnp.sum(spread, axis=1, keepdims=True), decay)
        dbc_out[rows, :STATE] = d_brows
        dbc_out[rows, STATE:] = d_crows
        decay_out[rows, :] = decay


def backward_carried(
    heads, block, cots, saved, factors, rate, kern, sent, blocks, near, weights, *refs,
):
    received = refs[:-4]
    cat_out, end_out, tail_out, scr = refs[-4:]
    length = cots.shape[0]
    width = heads * HEAD_DIM
    conv_width = width + 2 * STATE
    (dgate,) = columns(cots, width)
    act, scaled = columns(saved, conv_width, width)
    slope, step, run, sig = columns(factors, conv_width, LANES, LANES, LANES)
    _, states = columns(sent, width, width)
    u, dbc, decay = columns(near, width, 2 * STATE, LANES)
    strict = triangle(block, lambda i, j: i > j).astype(BF16)
    lane = lax.broadcasted_iota(jnp.int32, (block, LANES), 1)
    scr[0:PAD, :] = jnp.zeros((PAD, conv_width), F32)
    scr[PAD + length :, :] = jnp.zeros((PAD, conv_width), F32)
    cat_out[:, :width] = dgate[...]
    leaving = []
    for h in range(heads):
        total = jnp.zeros((HEAD_DIM, STATE), F32)
        for i, part in enumerate(received):
            total = total + weights[i * heads + h : i * heads + h + 1, :] * part[head(h), :]
        leaving.append(total)
    for k in reversed(range(length // block)):
        rows = slice(k * block, (k + 1) * block)
        into = slice(PAD + k * block, PAD + (k + 1) * block)
        r = run[rows, :]
        last = r[block - 1 : block, :]
        shrink = jnp.exp(last - r)
        whole = jnp.exp(last)
        b_rows = act[rows, width : width + STATE]
        d_brows = dbc[rows, :STATE]
        d_step = jnp.zeros((block, LANES), F32)
        for h in range(heads):
            at = k * heads + h
            here = slice(at * HEAD_DIM, (at + 1) * HEAD_DIM)
            cot_state = leaving[h].astype(BF16)
            past = shrink[:, h : h + 1] * dot(b_rows, cot_state, (1, 1))
            total = u[rows, head(h)] + past
            moved = scaled[rows, head(h)].astype(F32)
            d_brows = d_brows + dot((shrink[:, h : h + 1] * moved).astype(BF16), cot_state)
            kept = whole[:, h : h + 1] * leaving[h]
            constant = jnp.sum(
                jnp.sum(kept * states[rows, head(h)].astype(F32), axis=1, keepdims=True), axis=0, keepdims=True
            )
            spread = dot(strict, (moved * past).astype(BF16))
            d_decay = jnp.sum(spread, axis=1, keepdims=True) + constant + decay[rows, h : h + 1]
            direct = jnp.sum(act[rows, head(h)].astype(F32) * total, axis=1, keepdims=True)
            d_step = jnp.where(lane == h, direct - rate[:, h : h + 1] * d_decay, d_step)
            scr[into, head(h)] = step[rows, h : h + 1] * total * slope[rows, head(h)]
            leaving[h] = kept + blocks[here, :]
        scr[into, width : width + STATE] = d_brows * slope[rows, width : width + STATE]
        scr[into, width + STATE :] = dbc[rows, STATE:] * slope[rows, width + STATE :]
        cat_out[rows, width + conv_width :] = (d_step * sig[rows, :]).astype(BF16)
        value = kern[CONV - 1 : CONV, :] * scr[into, :]
        for j in range(1, CONV):
            value = value + kern[CONV - 1 - j : CONV - j, :] * scr[into.start + j : into.stop + j, :]
        cat_out[rows, width : width + conv_width] = value.astype(BF16)
        if k == length // block - 1:
            end_out[...] = value[block - PAD :, :]
    value = kern[CONV - 1 : CONV, :] * scr[0:PAD, :]
    for j in range(1, CONV):
        value = value + kern[CONV - 1 - j : CONV - j, :] * scr[j : PAD + j, :]
    tail_out[...] = value


def turned(value, axis, by):
    length = lax.axis_size(axis)
    return lax.ppermute(value, axis, [(i, (i + by) % length) for i in range(length)])


def paired(value, by):
    length = lax.axis_size("tp")
    return lax.ppermute(value, "tp", [(i, i ^ by) for i in range(length)])


def shifted(value, axis, by):
    length = lax.axis_size(axis)
    pairs = [(i, i + by) for i in range(length) if 0 <= i + by < length]
    return lax.ppermute(value, axis, pairs)


def after(value, token):
    columns = value.shape[1] if value.shape[1] <= token.shape[1] else 1
    return value + (token[:1, :columns] * 0).astype(value.dtype)


def halves(held):
    return ((0, held // 2), (held // 2, held - held // 2))


def ring_gather(parts, consume, result):
    chips = lax.axis_size("tp") // 2
    index = lax.axis_index("tp")
    chip, core = index // 2, index % 2
    arrived = []
    for step in range(chips):
        beside = [paired(part, 1) for part in parts]
        source = (chip - step) % chips
        owners = (source * 2 + core, source * 2 + 1 - core)
        if step < chips - 1:
            following = [turned(part, "tp", 2) for part in parts]
            result = consume(result, parts + beside, owners, None)
            parts = following
            arrived.append(parts)
        else:
            for i in range(len(parts)):
                result = consume(result, [parts[i], beside[i]], owners, i)
    return result, arrived


def multiply_into(weight, over, held, dtype):
    cuts = halves(held)

    def consume(result, rows, owners, only):
        product = dot(jnp.concatenate(rows, axis=0), weight, over).astype(dtype)
        at, size = (0, held) if only is None else cuts[only]
        for i, owner in enumerate(owners):
            piece = product[i * size : (i + 1) * size]
            result = lax.dynamic_update_slice(result, piece, (owner * held + at, 0))
        return result

    return consume


def product_rows(rows, weight, beside_out, mine_out):
    product = dot(rows[...], weight[...], (1, 1)).astype(BF16)
    count = beside_out.shape[0]
    beside_out[...] = product[:count]
    mine_out[...] = product[count:]


def multiply_rows(rows, weight):
    depth, inner = weight.shape
    block = math.gcd(depth, 1024)
    count = rows.shape[0] // 2
    out = pl.BlockSpec((count, block), lambda i: (0, i))
    return pl.pallas_call(
        product_rows,
        grid=(depth // block,),
        in_specs=[pl.BlockSpec(rows.shape, lambda i: (0, 0)), pl.BlockSpec((block, inner), lambda i: (i, 0))],
        out_specs=[out, out],
        out_shape=[shape(count, depth, dtype=BF16)] * 2,
        name="product_rows",
        compiler_params=pltpu.CompilerParams(vmem_limit_bytes=VMEM_LIMIT),
        cost_estimate=COST,
    )(rows, weight)


def ring_scatter(cat_parts, weight, held):
    chips = lax.axis_size("tp") // 2
    index = lax.axis_index("tp")
    chip, core = index // 2, index % 2
    inner = weight.shape[1]
    shares = []
    totals = []
    for cat, (at, size) in zip(cat_parts, halves(held)):
        rows = [
            lax.dynamic_slice(cat, ((((chip - 1 - step) % chips) * 2 + side) * held + at, 0), (size, inner))
            for side in (1 - core, core)
            for step in range(chips)
        ]
        other, own = multiply_rows(jnp.concatenate(rows, axis=0), weight)
        beside = paired(other, 1)
        shares.append((own, beside))
        totals.append((own[:size].astype(F32) + beside[:size].astype(F32)).astype(BF16))
    started = list(totals)
    for step in range(1, chips):
        for i, (at, size) in enumerate(halves(held)):
            own, beside = [share[step * size : (step + 1) * size].astype(F32) for share in shares[i]]
            if step == 1 and i == 0:
                own = after(own, started[1])
            totals[i] = (own + beside + turned(totals[i], "tp", 2).astype(F32)).astype(BF16)
    return jnp.concatenate(totals, axis=0)


def shape(*dims, dtype=F32):
    return jax.ShapeDtypeStruct(dims, dtype)


def body(
    normed_rows, out_grad, inner_weight, state_weight, step_weight, conv_inner, conv_state,
    step_bias, decay_log, norm_gain, out_weight,
):
    width = inner_weight.shape[2]
    heads = step_bias.shape[0]
    members = lax.axis_size("tp")
    shards = lax.axis_size("ctx")
    mine = lax.axis_index("ctx")
    length = normed_rows.shape[0] * members
    block = math.gcd(length, 128)
    count = length // block
    conv_width = width + 2 * STATE

    weight_cat = jnp.concatenate(
        [inner_weight[0], inner_weight[1], state_weight, jnp.pad(step_weight, ((0, 0), (0, LANES - heads)))],
        axis=1,
    )
    kern = jnp.concatenate([conv_inner, conv_state], axis=1)
    bias = jnp.pad(step_bias, (0, LANES - heads))[None]
    rate = jnp.pad(jnp.exp(decay_log), (0, LANES - heads))[None]
    gain = norm_gain[None]

    held, depth = normed_rows.shape
    cuts = halves(held)
    proj, rows_in = ring_gather(
        [normed_rows[at : at + size] for at, size in cuts],
        multiply_into(weight_cat, (1, 0), held, BF16),
        jnp.zeros((length, weight_cat.shape[1]), BF16),
    )
    local, grads_in = ring_gather(
        [after(out_grad[at : at + size], (rows_in[-2][1], rows_in[-1][0])[i] if len(rows_in) > 1 else rows_in[-1][i]) for i, (at, size) in enumerate(cuts)],
        multiply_into(out_weight, (1, 1), held, F32),
        jnp.zeros((length, width), F32),
    )

    tail = after(proj[length - PAD :, width : width + conv_width], grads_in[0][1])
    tail = after(shifted(tail, "ctx", 1), grads_in[0][0])
    saved, factors, diag, states, own = pl.pallas_call(
        partial(forward_local, heads, block),
        out_shape=[
            shape(length, conv_width + 3 * width, dtype=BF16),
            shape(length, conv_width + 3 * LANES),
            shape(length, width),
            shape(count * heads * HEAD_DIM, STATE),
            shape(heads * HEAD_DIM, STATE),
        ],
        scratch_shapes=[pltpu.VMEM((PAD + length, conv_width), F32)],
        name="forward_local",
        **PARAMS,
    )(proj, tail, kern, bias, rate)

    run = factors[:, conv_width + LANES : conv_width + 2 * LANES]
    ends = run.reshape(count, block, LANES)[:, block - 1, :heads]
    total_log = jnp.sum(ends, axis=0)
    message = jnp.concatenate([own, jnp.broadcast_to(jnp.pad(total_log, (0, LANES - heads)), (8, LANES))], axis=0)
    second = grads_in[min(1, len(grads_in) - 1)]
    message = after(message, second[1])
    received = [turned(message, "ctx", by) for by in range(1, shards)]
    logs = [part[heads * HEAD_DIM, :heads] for part in received]
    entering_weights = []
    between = jnp.zeros((heads,), F32)
    for by in range(1, shards):
        entering_weights.append(jnp.where(mine >= by, jnp.exp(between), 0.0))
        between = between + jnp.where(mine >= by, logs[by - 1], 0.0)
    leaving_weights = []
    between = jnp.zeros((heads,), F32)
    for by in range(1, shards):
        leaving_weights.append(jnp.where(mine + by < shards, jnp.exp(between), 0.0))
        between = between + jnp.where(mine + by < shards, logs[shards - by - 1], 0.0)

    def spread(parts):
        flat = jnp.concatenate(parts)
        return jnp.broadcast_to(flat[:, None], (flat.shape[0], LANES))

    gates, sent, squares = pl.pallas_call(
        partial(forward_carried, heads, block),
        out_shape=[
            shape(length, 3 * width),
            shape(length, 2 * width, dtype=BF16),
            shape(8, length),
        ],
        name="forward_carried",
        **PARAMS,
    )(proj, saved, factors, diag, states, after(spread(entering_weights), second[0]), *received)

    sums = pl.pallas_call(token_sums, out_shape=shape(8, length), name="token_sums", **PARAMS)(
        local, gain, gates, squares
    )

    sums = sums + paired(sums, 1)
    parts = [sums] + [turned(sums, "tp", by) for by in range(2, members, 2)]

    cots, blocks, own_cot = pl.pallas_call(
        partial(backward_gate, heads, block, width * members),
        out_shape=[
            shape(length, 3 * width, dtype=BF16),
            shape(count * heads * HEAD_DIM, STATE),
            shape(heads * HEAD_DIM, STATE),
        ],
        name="backward_gate",
        **PARAMS,
    )(local, gain, gates, saved, factors, *parts)

    returned = [turned(own_cot, "ctx", -by) for by in range(1, shards)]

    near = pl.pallas_call(
        partial(backward_local, heads, block),
        out_shape=shape(length, width + 2 * STATE + LANES),
        name="backward_local",
        **PARAMS,
    )(cots, saved, sent)

    cat, end, tail_cot = pl.pallas_call(
        partial(backward_carried, heads, block),
        out_shape=[
            shape(length, width + conv_width + LANES, dtype=BF16),
            shape(PAD, conv_width),
            shape(PAD, conv_width),
        ],
        scratch_shapes=[pltpu.VMEM((length + 2 * PAD, conv_width), F32)],
        name="backward_carried",
        **PARAMS,
    )(
        cots, saved, factors, rate, kern, sent, blocks, near,
        spread(leaving_weights), *returned,
    )

    incoming = shifted(tail_cot, "ctx", -1)
    whole = lax.dynamic_update_slice(cat, (end + incoming).astype(BF16), (length - PAD, width))
    return ring_scatter((cat, whole), weight_cat, held)


def solution(mesh):
    placed = (
        P(("ctx", "tp"), None),
        P(("ctx", "tp"), None),
        P(None, None, "tp"),
        P(),
        P(None, "tp"),
        P(None, "tp"),
        P(),
        P("tp"),
        P("tp"),
        P("tp"),
        P("tp", None),
    )
    return jax.shard_map(
        body, mesh=mesh, in_specs=placed, out_specs=P(("ctx", "tp"), None), check_vma=False
    )
```

```python
import math
from functools import partial

import jax
import jax.numpy as jnp
from jax import lax
from jax.experimental import pallas as pl
from jax.experimental.pallas import tpu as pltpu
from jax.sharding import PartitionSpec as P

HEAD_DIM = 128
STATE = 128
CONV = 4
LANES = 128
PAD = 8
EPSILON = 1e-05
EXACT = lax.Precision.HIGHEST
F32 = jnp.float32
BF16 = jnp.bfloat16
COST = pl.CostEstimate(flops=1000, bytes_accessed=1000, transcendentals=0)
VMEM_LIMIT = 16 * 1024 * 1024
PARAMS = dict(
    compiler_params=pltpu.CompilerParams(vmem_limit_bytes=16 * 1024 * 1024), cost_estimate=COST
)


def dot(a, b, over=(1, 0), precision=None):
    return lax.dot_general(
        a, b, (((over[0],), (over[1],)), ((), ())), precision=precision, preferred_element_type=F32
    )


def triangle(size, keep):
    rows = lax.broadcasted_iota(jnp.int32, (size, size), 0)
    columns = lax.broadcasted_iota(jnp.int32, (size, size), 1)
    return keep(rows, columns)


def head(h):
    return slice(h * HEAD_DIM, (h + 1) * HEAD_DIM)


def columns(ref, *widths):
    views = []
    first = 0
    for size in widths:
        views.append(ref.at[:, first : first + size])
        first = first + size
    return views


def forward_local(
    heads, block, proj, tail, kern, bias, rate,
    saved_out, factors_out, diag_out, states_out, own_out, ext,
):
    length = proj.shape[0]
    width = heads * HEAD_DIM
    conv_width = width + 2 * STATE
    act_out, scaled_out, decay_out, table_out = columns(saved_out, conv_width, width, width, width)
    slope_out, step_out, run_out, sig_out = columns(factors_out, conv_width, LANES, LANES, LANES)
    ext[0:PAD, :] = tail[...].astype(F32)
    ext[PAD:, :] = proj[:, width : width + conv_width].astype(F32)
    causal = triangle(block, lambda i, j: i >= j)
    lower = causal.astype(F32)
    state = [jnp.zeros((HEAD_DIM, STATE), F32) for _ in range(heads)]
    for k in range(length // block):
        rows = slice(k * block, (k + 1) * block)
        first = k * block + PAD - (CONV - 1)
        value = kern[0:1, :] * ext[first : first + block, :]
        for j in range(1, CONV):
            value = value + kern[j : j + 1, :] * ext[first + j : first + j + block, :]
        sigmoid = 1.0 / (1.0 + jnp.exp(-value))
        act = value * sigmoid
        act_out[rows, :] = act.astype(BF16)
        slope_out[rows, :] = sigmoid * (1.0 + value * (1.0 - sigmoid))
        raw = proj[rows, width + conv_width :].astype(F32) + bias[...]
        grown = jnp.exp(-jnp.abs(raw))
        step = jnp.maximum(raw, 0.0) + jnp.log1p(grown)
        step_out[rows, :] = step
        sig_out[rows, :] = jnp.where(raw >= 0.0, 1.0, grown) / (1.0 + grown)
        run = dot(lower, -step * rate[...], precision=EXACT)
        run_out[rows, :] = run
        run_t = run.T
        b_rows = act[:, width : width + STATE]
        c_rows = act[:, width + STATE :]
        scores = dot(c_rows, b_rows, (1, 1), EXACT)
        for h in range(heads):
            at = k * heads + h
            col = run[:, h : h + 1]
            decay = jnp.where(causal, jnp.exp(jnp.minimum(col - run_t[h : h + 1, :], 0.0)), 0.0)
            table = decay * scores
            scaled = act[:, head(h)] * step[:, h : h + 1]
            scaled_out[rows, head(h)] = scaled.astype(BF16)
            decay_out[rows, head(h)] = decay.astype(BF16)
            table_out[rows, head(h)] = table.astype(BF16)
            diag_out[rows, head(h)] = dot(table, scaled, precision=EXACT)
            states_out[at * HEAD_DIM : (at + 1) * HEAD_DIM, :] = state[h]
            last = run[block - 1 : block, h : h + 1]
            state[h] = jnp.exp(last) * state[h] + dot(
                jnp.exp(last - col) * scaled, b_rows, (0, 0), EXACT
            )
    for h in range(heads):
        own_out[head(h), :] = state[h]


def forward_carried(
    heads, block, proj, saved, factors, diag, states, weights, *refs,
):
    received = refs[:-3]
    gates_out, sent_out, sums_out = refs[-3:]
    length = proj.shape[0]
    width = heads * HEAD_DIM
    conv_width = width + 2 * STATE
    (act,) = columns(saved, conv_width)
    _, _, run = columns(factors, conv_width, LANES, LANES)
    gated_out, silu_out, slope_out = columns(gates_out, width, width, width)
    carried_out, states_out = columns(sent_out, width, width)
    entering = []
    for h in range(heads):
        total = jnp.zeros((HEAD_DIM, STATE), F32)
        for i, part in enumerate(received):
            total = total + weights[i * heads + h : i * heads + h + 1, :] * part[head(h), :]
        entering.append(total)
    base = jnp.zeros((1, LANES), F32)
    ones = jnp.ones((8, width), F32)
    for k in range(length // block):
        rows = slice(k * block, (k + 1) * block)
        r = run[rows, :]
        grow = jnp.exp(r)
        reach = jnp.exp(base)
        c_rows = act[rows, width + STATE :].astype(F32)
        for h in range(heads):
            at = k * heads + h
            here = slice(at * HEAD_DIM, (at + 1) * HEAD_DIM)
            state = states[here, :] + reach[:, h : h + 1] * entering[h]
            states_out[rows, head(h)] = state.astype(BF16)
            carried = grow[:, h : h + 1] * dot(c_rows, state, (1, 1), EXACT)
            carried_out[rows, head(h)] = carried.astype(BF16)
            out = diag[rows, head(h)] + carried
            gate = proj[rows, head(h)].astype(F32)
            sigmoid = 1.0 / (1.0 + jnp.exp(-gate))
            silu = gate * sigmoid
            silu_out[rows, head(h)] = silu
            gated_out[rows, head(h)] = out * silu
            slope_out[rows, head(h)] = out * sigmoid * (1.0 + gate * (1.0 - sigmoid))
        base = base + r[block - 1 : block, :]
        gated = gated_out[rows, :]
        sums_out[:, rows] = dot(ones, gated * gated, (1, 1), EXACT)


def token_sums(local, gain, gates, squares, sums_out):
    (gated,) = columns(gates, local.shape[1])
    ones = jnp.ones((8, local.shape[1]), F32)
    cross = dot(ones, gain[...] * local[...] * gated[...], (1, 1), EXACT)
    upper = lax.broadcasted_iota(jnp.int32, cross.shape, 0) < 4
    sums_out[...] = jnp.where(upper, squares[...], cross)


def backward_gate(heads, block, total_width, local, gain, gates, saved, factors, *refs):
    parts = refs[:-3]
    cots_out, blocks_out, own_out = refs[-3:]
    length = local.shape[0]
    width = heads * HEAD_DIM
    conv_width = width + 2 * STATE
    gated, silu, slope = columns(gates, width, width, width)
    (act,) = columns(saved, conv_width)
    _, _, run = columns(factors, conv_width, LANES, LANES)
    dgate_out, cot_out, grown_out = columns(cots_out, width, width, width)
    pick = lax.broadcasted_iota(jnp.int32, (8, LANES), 0)
    own = [jnp.zeros((HEAD_DIM, STATE), F32) for _ in range(heads)]
    base = jnp.zeros((1, LANES), F32)
    for k in range(length // block):
        rows = slice(k * block, (k + 1) * block)
        sums = parts[0][:, rows]
        for part in parts[1:]:
            sums = sums + part[:, rows]
        square = dot(sums, (pick == 0).astype(F32), (0, 0), EXACT) / total_width
        cross = dot(sums, (pick == 4).astype(F32), (0, 0), EXACT) / total_width
        inverse = lax.rsqrt(square + EPSILON)
        cross = cross * (inverse * inverse * inverse)
        r = run[rows, :]
        grow = jnp.exp(r)
        reach = jnp.exp(base)
        c_rows = act[rows, width + STATE :]
        for h in range(heads):
            at = k * heads + h
            d_gated = inverse * (gain[:, head(h)] * local[rows, head(h)]) - gated[rows, head(h)] * cross
            dgate_out[rows, head(h)] = (d_gated * slope[rows, head(h)]).astype(BF16)
            cot = d_gated * silu[rows, head(h)]
            cot_out[rows, head(h)] = cot.astype(BF16)
            grown = (grow[:, h : h + 1] * cot).astype(BF16)
            grown_out[rows, head(h)] = grown
            entering = dot(grown, c_rows, (0, 0))
            blocks_out[at * HEAD_DIM : (at + 1) * HEAD_DIM, :] = entering
            own[h] = own[h] + reach[:, h : h + 1] * entering
        base = base + r[block - 1 : block, :]
    for h in range(heads):
        own_out[head(h), :] = own[h]


def backward_local(heads, block, cots, saved, sent, near_out):
    length = cots.shape[0]
    width = heads * HEAD_DIM
    _, cot, grown = columns(cots, width, width, width)
    act, scaled, decays, table = columns(saved, width + 2 * STATE, width, width, width)
    carried, states = columns(sent, width, width)
    u_out, dbc_out, decay_out = columns(near_out, width, 2 * STATE, LANES)
    before = triangle(block, lambda i, j: i > j)
    upper = triangle(block, lambda i, j: i <= j).astype(BF16)
    lane = lax.broadcasted_iota(jnp.int32, (block, LANES), 1)
    for k in range(length // block):
        rows = slice(k * block, (k + 1) * block)
        b_rows = act[rows, width : width + STATE]
        c_rows = act[rows, width + STATE :]
        d_brows = jnp.zeros((block, STATE), F32)
        d_crows = jnp.zeros((block, STATE), F32)
        decay = jnp.zeros((block, LANES), F32)
        for h in range(heads):
            g = cot[rows, head(h)]
            weights = table[rows, head(h)]
            inner = dot(g, scaled[rows, head(h)], (1, 1))
            pairs = (decays[rows, head(h)].astype(F32) * inner).astype(BF16)
            mixed = (weights.astype(F32) * inner).astype(BF16)
            d_crows = d_crows + dot(pairs, b_rows)
            d_crows = d_crows + dot(grown[rows, head(h)], states[rows, head(h)])
            d_brows = d_brows + dot(pairs, c_rows, (0, 0))
            u_out[rows, head(h)] = dot(weights, g, (0, 0))
            through = (g.astype(F32) * carried[rows, head(h)].astype(F32)).astype(BF16)
            spread = jnp.where(before, dot(upper, mixed), 0.0) + dot(upper, through)
            decay = jnp.where(lane == h, jnp.sum(spread, axis=1, keepdims=True), decay)
        dbc_out[rows, :STATE] = d_brows
        dbc_out[rows, STATE:] = d_crows
        decay_out[rows, :] = decay


def backward_carried(
    heads, block, cots, saved, factors, rate, kern, sent, blocks, near, weights, *refs,
):
    received = refs[:-4]
    cat_out, end_out, tail_out, scr = refs[-4:]
    length = cots.shape[0]
    width = heads * HEAD_DIM
    conv_width = width + 2 * STATE
    (dgate,) = columns(cots, width)
    act, scaled = columns(saved, conv_width, width)
    slope, step, run, sig = columns(factors, conv_width, LANES, LANES, LANES)
    _, states = columns(sent, width, width)
    u, dbc, decay = columns(near, width, 2 * STATE, LANES)
    strict = triangle(block, lambda i, j: i > j).astype(BF16)
    lane = lax.broadcasted_iota(jnp.int32, (block, LANES), 1)
    scr[0:PAD, :] = jnp.zeros((PAD, conv_width), F32)
    scr[PAD + length :, :] = jnp.zeros((PAD, conv_width), F32)
    cat_out[:, :width] = dgate[...]
    leaving = []
    for h in range(heads):
        total = jnp.zeros((HEAD_DIM, STATE), F32)
        for i, part in enumerate(received):
            total = total + weights[i * heads + h : i * heads + h + 1, :] * part[head(h), :]
        leaving.append(total)
    for k in reversed(range(length // block)):
        rows = slice(k * block, (k + 1) * block)
        into = slice(PAD + k * block, PAD + (k + 1) * block)
        r = run[rows, :]
        last = r[block - 1 : block, :]
        shrink = jnp.exp(last - r)
        whole = jnp.exp(last)
        b_rows = act[rows, width : width + STATE]
        d_brows = dbc[rows, :STATE]
        d_step = jnp.zeros((block, LANES), F32)
        for h in range(heads):
            at = k * heads + h
            here = slice(at * HEAD_DIM, (at + 1) * HEAD_DIM)
            cot_state = leaving[h].astype(BF16)
            past = shrink[:, h : h + 1] * dot(b_rows, cot_state, (1, 1))
            total = u[rows, head(h)] + past
            moved = scaled[rows, head(h)].astype(F32)
            d_brows = d_brows + dot((shrink[:, h : h + 1] * moved).astype(BF16), cot_state)
            kept = whole[:, h : h + 1] * leaving[h]
            constant = jnp.sum(
                jnp.sum(kept * states[rows, head(h)].astype(F32), axis=1, keepdims=True), axis=0, keepdims=True
            )
            spread = dot(strict, (moved * past).astype(BF16))
            d_decay = jnp.sum(spread, axis=1, keepdims=True) + constant + decay[rows, h : h + 1]
            direct = jnp.sum(act[rows, head(h)].astype(F32) * total, axis=1, keepdims=True)
            d_step = jnp.where(lane == h, direct - rate[:, h : h + 1] * d_decay, d_step)
            scr[into, head(h)] = step[rows, h : h + 1] * total * slope[rows, head(h)]
            leaving[h] = kept + blocks[here, :]
        scr[into, width : width + STATE] = d_brows * slope[rows, width : width + STATE]
        scr[into, width + STATE :] = dbc[rows, STATE:] * slope[rows, width + STATE :]
        cat_out[rows, width + conv_width :] = (d_step * sig[rows, :]).astype(BF16)
        value = kern[CONV - 1 : CONV, :] * scr[into, :]
        for j in range(1, CONV):
            value = value + kern[CONV - 1 - j : CONV - j, :] * scr[into.start + j : into.stop + j, :]
        cat_out[rows, width : width + conv_width] = value.astype(BF16)
        if k == length // block - 1:
            end_out[...] = value[block - PAD :, :]
    value = kern[CONV - 1 : CONV, :] * scr[0:PAD, :]
    for j in range(1, CONV):
        value = value + kern[CONV - 1 - j : CONV - j, :] * scr[j : PAD + j, :]
    tail_out[...] = value


def turned(value, axis, by):
    length = lax.axis_size(axis)
    return lax.ppermute(value, axis, [(i, (i + by) % length) for i in range(length)])


def paired(value, by):
    length = lax.axis_size("tp")
    return lax.ppermute(value, "tp", [(i, i ^ by) for i in range(length)])


def shifted(value, axis, by):
    length = lax.axis_size(axis)
    pairs = [(i, i + by) for i in range(length) if 0 <= i + by < length]
    return lax.ppermute(value, axis, pairs)


def after(value, token):
    columns = value.shape[1] if value.shape[1] <= token.shape[1] else 1
    return value + (token[:1, :columns] * 0).astype(value.dtype)


def halves(held):
    return ((0, held // 2), (held // 2, held - held // 2))


def ring_gather(parts, consume, result):
    chips = lax.axis_size("tp") // 2
    index = lax.axis_index("tp")
    chip, core = index // 2, index % 2
    arrived = []
    for step in range(chips):
        beside = [paired(part, 1) for part in parts]
        source = (chip - step) % chips
        owners = (source * 2 + core, source * 2 + 1 - core)
        if step < chips - 1:
            following = [turned(part, "tp", 2) for part in parts]
            result = consume(result, parts + beside, owners, None)
            parts = following
            arrived.append(parts)
        else:
            for i in range(len(parts)):
                result = consume(result, [parts[i], beside[i]], owners, i)
    return result, arrived


def multiply_into(weight, over, held, dtype):
    cuts = halves(held)

    def consume(result, rows, owners, only):
        product = dot(jnp.concatenate(rows, axis=0), weight, over).astype(dtype)
        at, size = (0, held) if only is None else cuts[only]
        for i, owner in enumerate(owners):
            piece = product[i * size : (i + 1) * size]
            result = lax.dynamic_update_slice(result, piece, (owner * held + at, 0))
        return result

    return consume


def product_rows(rows, weight, beside_out, mine_out):
    product = dot(rows[...], weight[...], (1, 1)).astype(BF16)
    count = beside_out.shape[0]
    beside_out[...] = product[:count]
    mine_out[...] = product[count:]


def multiply_rows(rows, weight):
    depth, inner = weight.shape
    block = math.gcd(depth, 1024)
    count = rows.shape[0] // 2
    out = pl.BlockSpec((count, block), lambda i: (0, i))
    return pl.pallas_call(
        product_rows,
        grid=(depth // block,),
        in_specs=[pl.BlockSpec(rows.shape, lambda i: (0, 0)), pl.BlockSpec((block, inner), lambda i: (i, 0))],
        out_specs=[out, out],
        out_shape=[shape(count, depth, dtype=BF16)] * 2,
        name="product_rows",
        compiler_params=pltpu.CompilerParams(vmem_limit_bytes=VMEM_LIMIT),
        cost_estimate=COST,
    )(rows, weight)


def ring_scatter(cat_parts, weight, held):
    chips = lax.axis_size("tp") // 2
    index = lax.axis_index("tp")
    chip, core = index // 2, index % 2
    inner = weight.shape[1]
    shares = []
    totals = []
    for cat, (at, size) in zip(cat_parts, halves(held)):
        rows = [
            lax.dynamic_slice(cat, ((((chip - 1 - step) % chips) * 2 + side) * held + at, 0), (size, inner))
            for side in (1 - core, core)
            for step in range(chips)
        ]
        other, own = multiply_rows(jnp.concatenate(rows, axis=0), weight)
        beside = paired(other, 1)
        shares.append((own, beside))
        totals.append((own[:size].astype(F32) + beside[:size].astype(F32)).astype(BF16))
    started = list(totals)
    for step in range(1, chips):
        for i, (at, size) in enumerate(halves(held)):
            own, beside = [share[step * size : (step + 1) * size].astype(F32) for share in shares[i]]
            if step == 1 and i == 0:
                own = after(own, started[1])
            totals[i] = (own + beside + turned(totals[i], "tp", 2).astype(F32)).astype(BF16)
    return jnp.concatenate(totals, axis=0)


def shape(*dims, dtype=F32):
    return jax.ShapeDtypeStruct(dims, dtype)


def body(
    normed_rows, out_grad, inner_weight, state_weight, step_weight, conv_inner, conv_state,
    step_bias, decay_log, norm_gain, out_weight,
):
    width = inner_weight.shape[2]
    heads = step_bias.shape[0]
    members = lax.axis_size("tp")
    shards = lax.axis_size("ctx")
    mine = lax.axis_index("ctx")
    length = normed_rows.shape[0] * members
    block = math.gcd(length, 128)
    count = length // block
    conv_width = width + 2 * STATE

    weight_cat = jnp.concatenate(
        [inner_weight[0], inner_weight[1], state_weight, jnp.pad(step_weight, ((0, 0), (0, LANES - heads)))],
        axis=1,
    )
    kern = jnp.concatenate([conv_inner, conv_state], axis=1)
    bias = jnp.pad(step_bias, (0, LANES - heads))[None]
    rate = jnp.pad(jnp.exp(decay_log), (0, LANES - heads))[None]
    gain = norm_gain[None]

    held, depth = normed_rows.shape
    cuts = halves(held)
    proj, rows_in = ring_gather(
        [normed_rows[at : at + size] for at, size in cuts],
        multiply_into(weight_cat, (1, 0), held, BF16),
        jnp.zeros((length, weight_cat.shape[1]), BF16),
    )
    local, grads_in = ring_gather(
        [after(out_grad[at : at + size], (rows_in[-2][1], rows_in[-1][0])[i] if len(rows_in) > 1 else rows_in[-1][i]) for i, (at, size) in enumerate(cuts)],
        multiply_into(out_weight, (1, 1), held, F32),
        jnp.zeros((length, width), F32),
    )

    tail = after(proj[length - PAD :, width : width + conv_width], grads_in[0][1])
    tail = after(shifted(tail, "ctx", 1), grads_in[0][0])
    saved, factors, diag, states, own = pl.pallas_call(
        partial(forward_local, heads, block),
        out_shape=[
            shape(length, conv_width + 3 * width, dtype=BF16),
            shape(length, conv_width + 3 * LANES),
            shape(length, width),
            shape(count * heads * HEAD_DIM, STATE),
            shape(heads * HEAD_DIM, STATE),
        ],
        scratch_shapes=[pltpu.VMEM((PAD + length, conv_width), F32)],
        name="forward_local",
        **PARAMS,
    )(proj, tail, kern, bias, rate)

    run = factors[:, conv_width + LANES : conv_width + 2 * LANES]
    ends = run.reshape(count, block, LANES)[:, block - 1, :heads]
    total_log = jnp.sum(ends, axis=0)
    message = jnp.concatenate([own, jnp.broadcast_to(jnp.pad(total_log, (0, LANES - heads)), (8, LANES))], axis=0)
    second = grads_in[min(1, len(grads_in) - 1)]
    third = grads_in[min(2, len(grads_in) - 1)]
    message = after(message, second[1])
    received = [turned(message, "ctx", by) for by in range(1, shards)]
    logs = [part[heads * HEAD_DIM, :heads] for part in received]
    entering_weights = []
    between = jnp.zeros((heads,), F32)
    for by in range(1, shards):
        entering_weights.append(jnp.where(mine >= by, jnp.exp(between), 0.0))
        between = between + jnp.where(mine >= by, logs[by - 1], 0.0)
    leaving_weights = []
    between = jnp.zeros((heads,), F32)
    for by in range(1, shards):
        leaving_weights.append(jnp.where(mine + by < shards, jnp.exp(between), 0.0))
        between = between + jnp.where(mine + by < shards, logs[shards - by - 1], 0.0)

    def spread(parts):
        flat = jnp.concatenate(parts)
        return jnp.broadcast_to(flat[:, None], (flat.shape[0], LANES))

    gates, sent, squares = pl.pallas_call(
        partial(forward_carried, heads, block),
        out_shape=[
            shape(length, 3 * width),
            shape(length, 2 * width, dtype=BF16),
            shape(8, length),
        ],
        name="forward_carried",
        **PARAMS,
    )(proj, saved, factors, diag, states, after(after(spread(entering_weights), second[0]), third[0]), *received)

    sums = pl.pallas_call(token_sums, out_shape=shape(8, length), name="token_sums", **PARAMS)(
        local, gain, gates, squares
    )

    sums = sums + paired(sums, 1)
    parts = [sums] + [turned(sums, "tp", by) for by in range(2, members, 2)]

    cots, blocks, own_cot = pl.pallas_call(
        partial(backward_gate, heads, block, width * members),
        out_shape=[
            shape(length, 3 * width, dtype=BF16),
            shape(count * heads * HEAD_DIM, STATE),
            shape(heads * HEAD_DIM, STATE),
        ],
        name="backward_gate",
        **PARAMS,
    )(local, gain, gates, saved, factors, *parts)

    returned = [turned(own_cot, "ctx", -by) for by in range(1, shards)]

    near = pl.pallas_call(
        partial(backward_local, heads, block),
        out_shape=shape(length, width + 2 * STATE + LANES),
        name="backward_local",
        **PARAMS,
    )(cots, saved, sent)

    cat, end, tail_cot = pl.pallas_call(
        partial(backward_carried, heads, block),
        out_shape=[
            shape(length, width + conv_width + LANES, dtype=BF16),
            shape(PAD, conv_width),
            shape(PAD, conv_width),
        ],
        scratch_shapes=[pltpu.VMEM((length + 2 * PAD, conv_width), F32)],
        name="backward_carried",
        **PARAMS,
    )(
        cots, saved, factors, rate, kern, sent, blocks, near,
        spread(leaving_weights), *returned,
    )

    incoming = shifted(tail_cot, "ctx", -1)
    whole = lax.dynamic_update_slice(cat, (end + incoming).astype(BF16), (length - PAD, width))
    return ring_scatter((cat, whole), weight_cat, held)


def solution(mesh):
    placed = (
        P(("ctx", "tp"), None),
        P(("ctx", "tp"), None),
        P(None, None, "tp"),
        P(),
        P(None, "tp"),
        P(None, "tp"),
        P(),
        P("tp"),
        P("tp"),
        P("tp"),
        P("tp", None),
    )
    return jax.shard_map(
        body, mesh=mesh, in_specs=placed, out_specs=P(("ctx", "tp"), None), check_vma=False
    )
```
